128 devices in a mesh: tx: 8 (over y, core), brick: 16 (over x, z).
Axes of the slice: x: 4, y: 4, z: 4, core: 2. Of those that a mesh axis runs over, the one named last changes fastest.
Arguments:
- fields: float32 [8, 2, 2, 3, 128, 64, 128], P('tx', None, None, None, 'brick'), may hold values from -6 to 6
- sources: float32 [8, 2, 2, 3, 128, 64, 128], P('tx', None, None, None, 'brick'), may hold values from -6 to 6
- conductivity: float32 [8, 128, 64, 128], P('tx', 'brick'), may hold values from 0.1 to 1.5
- omegas: float32 [2], replicated, may hold values from 0.4 to 2
- tx_bricks: int32 [8], replicated, may hold values from 6 to 16, as said below
- owner_map: int32 [128], replicated, may hold values from 0 to 127, each once
- row_brick: int32 [8, 8192, 1], P('tx', 'brick'), may hold values from 0 to 127; in each aligned block of 512 rows (0 to 511, 512 to 1023, ..., all dimensions but the last counted through in order) at most 8 rows name the same one
- row_offset: int32 [8, 8192], P('tx', 'brick'), may hold values from 0 to 31
Outputs:
- grid_gradient: float32 [4096, 128], P(('tx', 'brick'))
The draws below stay inside these ranges and needn't reach their ends.
Inputs may be any that keep to these rules, and one draw needn't show every extreme that they name: `tx_bricks`: every transmitter occupies between a third and all of its group; some transmitter occupies all 16 and some the fewest. `row_brick`: within the rows of one device no brick is named more than 8 times, a bound that some block reaches.
All inputs are finite; a program needn't handle non-finite values.
Results may differ from the reference program's by a relative error of at most 0.0001.
Values sent between devices are 32-bit elements; how exact they have to be, the bound alone decides.
No kernel may reach another device: no remote copies, remote signals or barrier semaphores. Data moves between devices by JAX's collectives and lax.ppermute only.
A program may use at most 64 MiB of HBM per device.

```python
import math
import jax
import jax.numpy as jnp
import numpy as np
from jax import lax

CXL = 8
CY = 64
CZ = 128
NF = 2
G_DEV = 32
NTX = 8
NXL = 128
CAP = 8
DEVICES = 128


def draw_tx_bricks(key, part):
    key = jax.random.fold_in(key, 7)
    first_key, second_key = jax.random.split(key)
    bricks_total = NXL // CXL
    fewest = (bricks_total + 2) // 3
    counts = jax.random.randint(first_key, (NTX,), fewest, bricks_total + 1)
    ranking = jax.random.permutation(second_key, NTX)
    counts = counts.at[ranking[0]].set(bricks_total).at[ranking[1]].set(fewest)
    return counts.astype(jnp.int32)


def plant(array, rng, least, largest):
    longest = array.shape.index(max(array.shape))
    spots = []
    for shift in (0, 1):
        where = [jax.random.randint(jax.random.fold_in(rng, axis), (), 0, length) for axis, length in enumerate(array.shape)]
        where[longest] = (where[longest] + shift) % array.shape[longest]
        spots.append(tuple(where))
    return array.at[spots[0]].set(least).at[spots[1]].set(largest)


def block_levels(own_key, dims, cuts, least, high):
    factor_of = 1.0
    for position, blocks in cuts:
        heights = jax.random.uniform(jax.random.fold_in(jax.random.fold_in(own_key, 6), position), (blocks,), jnp.float32, least / len(cuts), high / len(cuts))
        factor_of = factor_of * jnp.repeat(jnp.exp(heights), dims[position] // blocks).reshape((-1,) + (1,) * (len(dims) - 1 - position))
    return factor_of


def shared_out(stream_key, own, number, rows, number_of, top, bound, slope):
    sequence = jax.random.permutation(stream_key, number_of)
    crowded, ordinary = load_shares(number_of, rows * top, bound, slope, True), load_shares(number_of, rows * top, bound, slope, False)
    places = jnp.arange(number_of)

    def named(lengths, offset_by):
        used = int((lengths > 0).sum())
        fixed = max(1, used // 4)
        shifted = fixed + (places - fixed + offset_by * (used - fixed)) % max(1, number_of - fixed)
        return jnp.zeros((number_of,), jnp.int32).at[sequence[jnp.where(places < fixed, places, shifted)]].set(jnp.asarray(lengths, jnp.int32))

    lengths = jnp.where(number % 4 == 0, named(crowded, number // 4), named(ordinary, number - number // 4 - 1))
    mixed = jax.random.permutation(jax.random.fold_in(own, 3), number_of)
    giver, receiver = mixed[0:number_of // 2 * 2:2], mixed[1:number_of // 2 * 2:2]
    margin = jnp.minimum(lengths[giver] - 1, bound - lengths[receiver]) // 2
    margin = jnp.where((giver == sequence[0]) | (receiver == sequence[0]) | (lengths[receiver] == 0), 0, jnp.maximum(margin, 0))
    shifted = jax.random.randint(jax.random.fold_in(own, 4), (number_of // 2,), 0, 1 << 20) % (margin + 1)
    lengths = lengths.at[giver].add(-shifted).at[receiver].add(shifted)
    items = jnp.searchsorted(jnp.cumsum(lengths), jnp.arange(rows * top), side="right").astype(jnp.int32)
    listing = items.reshape(top, rows).T
    listing = listing[jax.random.permutation(jax.random.fold_in(own, 1), rows)]
    offset_by = jax.random.randint(jax.random.fold_in(own, 2), (rows, 1), 0, top)
    return jnp.take_along_axis(listing, (jnp.arange(top)[None, :] + offset_by) % top, axis=1)


def load_shares(count, total, bound, skew, full):
    portions = [(1 << 20) // math.isqrt(grade ** skew) + 1 for grade in range(1, count + 1)]
    largest = bound if full else min(bound, max(-(-total // count), total * portions[0] // sum(portions)))
    least = 1 if total - largest >= count - 1 else 0
    given, rest = [largest] + [least] * (count - 1), total - largest - least * (count - 1)
    while rest > 0:
        free = [i for i in range(1, count) if given[i] < largest] or [i for i in range(1, count) if given[i] < bound]
        mass, budget = sum([portions[i] for i in free]), rest
        for i in free:
            extra = min(bound - given[i], max(1, budget * portions[i] // mass), rest)
            given[i] = given[i] + extra
            rest = rest - extra
    return np.array(given)


def scatter_about(stream_key, extent, deviation, most, cuts=(), kind=jnp.bfloat16):
    drawn = jax.random.normal(stream_key, extent, jnp.float32) * deviation
    if len(cuts) > 0:
        drawn = block_levels(stream_key, extent, cuts, -0.22, 0.18) * drawn
    return jnp.clip(drawn, min=-most, max=most).astype(kind)


def setup_inputs(seed: int = 0) -> dict:
    splits = jax.random.split(jax.random.key(seed), 9)
    fields = scatter_about(splits[0], (NTX, NF, 2, 3, NXL, CY, CZ), 1.0, 6.0, ((0, 8), (4, 16)), jnp.float32)
    sources = scatter_about(splits[1], (NTX, NF, 2, 3, NXL, CY, CZ), 1.0, 6.0, ((0, 8), (4, 16)), jnp.float32)
    conductivity = jnp.clip(jnp.exp(math.log(1.5) - 2.7080502 * jax.random.uniform(splits[2], (NTX, NXL, CY, CZ), jnp.float32) ** block_levels(splits[2], (NTX, NXL, CY, CZ), ((0, 8), (1, 16)), -0.2, 0.2)), 0.1, 1.5)
    omegas = jnp.clip(jnp.exp(jax.random.uniform(splits[3], (NF,), jnp.float32, math.log(0.4), math.log(2.0))), 0.4, 2.0)
    tx_bricks = draw_tx_bricks(jax.random.fold_in(splits[8], 71), 0)
    owner_map = jax.random.permutation(splits[5], DEVICES).astype(jnp.int32)
    row_brick_keys = jax.random.split(jax.random.fold_in(splits[6], 1), NTX * (NXL * CY) // (CXL * CY))
    row_brick_turns = jax.random.permutation(jax.random.fold_in(splits[6], 3), NTX * (NXL * CY) // (CXL * CY))
    row_brick = jax.vmap(lambda own, number: shared_out(jax.random.fold_in(splits[6], 2), own, number, CXL * CY, DEVICES, 1, CAP, 2))(row_brick_keys, row_brick_turns).reshape((NTX, NXL * CY, 1))
    row_offset = plant(jax.random.randint(splits[7], (NTX, NXL * CY), 0, G_DEV), jax.random.fold_in(splits[7], 1), 0, G_DEV - 1).astype(jnp.int32)
    return dict(fields=fields, sources=sources, conductivity=conductivity, omegas=omegas, tx_bricks=tx_bricks, owner_map=owner_map, row_brick=row_brick, row_offset=row_offset)


def shift_next(values, axis):
    count = values.shape[axis]
    return jnp.concatenate([lax.slice_in_dim(values, 1, count, axis=axis), jnp.zeros_like(lax.slice_in_dim(values, 0, 1, axis=axis))], axis=axis)


def shift_prev(values, axis):
    count = values.shape[axis]
    return jnp.concatenate([jnp.zeros_like(lax.slice_in_dim(values, 0, 1, axis=axis)), lax.slice_in_dim(values, 0, count - 1, axis=axis)], axis=axis)


def diff_forward(values, axis):
    return shift_next(values, axis) - values


def diff_backward(values, axis):
    return values - shift_prev(values, axis)


def curl_with(field, differ):
    comp_x = field[..., 0, :, :, :]
    comp_y = field[..., 1, :, :, :]
    comp_z = field[..., 2, :, :, :]
    rank = comp_x.ndim
    ax_x, ax_y, ax_z = rank - 3, rank - 2, rank - 1
    out_x = differ(comp_z, ax_y) - differ(comp_y, ax_z)
    out_y = differ(comp_x, ax_z) - differ(comp_z, ax_x)
    out_z = differ(comp_y, ax_x) - differ(comp_x, ax_y)
    return jnp.stack([out_x, out_y, out_z], axis=rank - 3)


def operator(field, conduct, omegas):
    curled = curl_with(curl_with(field, diff_forward), diff_backward)
    rotated = jnp.stack([-field[:, 1], field[:, 0]], axis=1)
    return curled + omegas[:, None, None, None, None, None] * conduct * rotated


def reference(fields, sources, conductivity, omegas, tx_bricks, owner_map, row_brick, row_offset):
    planes = jnp.arange(NXL, dtype=jnp.int32)
    grid = jnp.zeros((DEVICES * G_DEV, CZ), jnp.float32)
    for trans in range(NTX):
        active = (planes < tx_bricks[trans] * CXL).astype(jnp.float32)[:, None, None]
        efield = fields[trans] * active
        residual = (operator(efield, conductivity[trans], omegas) - sources[trans]) * active
        adjoint = operator(residual, conductivity[trans], omegas) * active
        terms = efield[:, 0] * adjoint[:, 1] - efield[:, 1] * adjoint[:, 0]
        local = 0.003 * jnp.sum(omegas[:, None, None, None, None] * terms, axis=(0, 1))
        local_rows = local.reshape(NXL * CY, CZ)
        target = owner_map[row_brick[trans, :, 0]] * G_DEV + row_offset[trans]
        grid = grid.at[target].add(local_rows)
    return grid
```

```python
import jax
import jax.numpy as jnp
from jax import lax
from jax.experimental import pallas as pl
from jax.experimental.pallas import tpu as pltpu
from jax.sharding import PartitionSpec as P

PL, NY, NZ, NF = 8, 64, 128, 2
ROWS = PL * NY
G_DEV = 32
CAP = 8
DEV = 128
SLOTS = CAP + 1
TX, BRICK = 8, 16
F32, BF16, I32 = jnp.float32, jnp.bfloat16, jnp.int32
SCALE = 0.003


def next_y(v):
    rows = lax.broadcasted_iota(I32, v.shape, 0)
    return jnp.where(rows == NY - 1, 0.0, pltpu.roll(v, NY - 1, 0))


def prev_y(v):
    rows = lax.broadcasted_iota(I32, v.shape, 0)
    return jnp.where(rows == 0, 0.0, pltpu.roll(v, 1, 0))


def next_z(v):
    lanes = lax.broadcasted_iota(I32, v.shape, 1)
    return jnp.where(lanes == NZ - 1, 0.0, pltpu.roll(v, NZ - 1, 1))


def prev_z(v):
    lanes = lax.broadcasted_iota(I32, v.shape, 1)
    return jnp.where(lanes == 0, 0.0, pltpu.roll(v, 1, 1))


def fy(v):
    return next_y(v) - v


def by(v):
    return v - prev_y(v)


def fz(v):
    return next_z(v) - v


def bz(v):
    return v - prev_z(v)


def q_of(vx, vy, vz):
    return fz(vx) + vz, vy + fy(vx)


def rotate_add(part, weight, other):
    return -(weight * other) if part == 0 else weight * other


def payload_kernel(om_ref, elo_ref, ehi_ref, slo_ref, shi_ref, clo_ref, chi_ref, up_ref, dn_ref):
    for f in range(NF):
        om = om_ref[f]
        for part in range(2):
            ch = 2 * f + part
            vx, vy, vz = (elo_ref[0, f, part, c, 0] for c in range(3))
            hx = fy(vz) - fz(vy)
            hy = fz(vx) - (elo_ref[0, f, part, 2, 1] - vz)
            hz = (elo_ref[0, f, part, 1, 1] - vy) - fy(vx)
            w = om * clo_ref[0, 0]
            ry = bz(hx) - hz + rotate_add(part, w, elo_ref[0, f, 1 - part, 1, 0]) - slo_ref[0, f, part, 1, 0]
            rz = hy - by(hx) + rotate_add(part, w, elo_ref[0, f, 1 - part, 2, 0]) - slo_ref[0, f, part, 2, 0]
            dn_ref[2 * ch] = vy
            dn_ref[2 * ch + 1] = vz
            dn_ref[8 + 2 * ch] = ry
            dn_ref[8 + 2 * ch + 1] = rz
            ux, uy, uz = (ehi_ref[0, f, part, c, 0] for c in range(3))
            vx, vy, vz = (ehi_ref[0, f, part, c, 1] for c in range(3))
            qy, qz = q_of(vx, vy, vz)
            hx = fy(vz) - fz(vy)
            hy = qy
            hz = -qz
            gy = fz(ux) - (vz - uz)
            gz = (vy - uy) - fy(ux)
            w = om * chi_ref[0, 0]
            o = [ehi_ref[0, f, 1 - part, c, 1] for c in range(3)]
            rx = by(hz) - bz(hy) + rotate_add(part, w, o[0]) - shi_ref[0, f, part, 0, 0]
            ry = bz(hx) - (hz - gz) + rotate_add(part, w, o[1]) - shi_ref[0, f, part, 1, 0]
            rz = (hy - gy) - by(hx) + rotate_add(part, w, o[2]) - shi_ref[0, f, part, 2, 0]
            sy, sz = q_of(rx, ry, rz)
            up_ref[2 * ch] = qy
            up_ref[2 * ch + 1] = qz
            up_ref[8 + 2 * ch] = sy
            up_ref[8 + 2 * ch + 1] = sz


def one_hot(cond):
    return jnp.where(cond, 1.0, 0.0).astype(BF16)


def split3(v):
    hi = v.astype(BF16)
    rest = v - hi.astype(F32)
    mid = rest.astype(BF16)
    low = (rest - mid.astype(F32)).astype(BF16)
    return hi, mid, low


def dot(a, b):
    return jnp.dot(a, b, preferred_element_type=F32)


def exact_dot(hot, v):
    hi, mid, low = split3(v)
    return dot(hot, hi) + (dot(hot, mid) + dot(hot, low))


def active_of(tb_ref):
    brick = lax.axis_index("brick")
    span = tb_ref[lax.axis_index("tx")]
    return brick, span


def main_kernel(om_ref, tb_ref, e_ref, s_ref, c_ref, rb_ref, ro_ref, own_ref, out_ref, slot_ref, r_ref, h_ref, loc_ref):
    brick, span = active_of(tb_ref)
    live = jnp.where(brick < span, 1.0, 0.0).astype(F32)
    zero = jnp.zeros((NY, NZ), F32)
    for i in range(12):
        r_ref[i, PL] = zero
    for i in range(8):
        h_ref[i] = zero

    def first(p, carry):
        q = jnp.minimum(p + 1, PL - 1)
        inside = jnp.where(p < PL - 1, 1.0, 0.0).astype(F32)
        sig = c_ref[0, p]
        for f in range(NF):
            w = om_ref[f] * sig
            for part in range(2):
                ch = 2 * f + part
                vx, vy, vz = (e_ref[0, f, part, c, p] for c in range(3))
                ny = e_ref[0, f, part, 1, q] * inside
                nz = e_ref[0, f, part, 2, q] * inside
                hx = fy(vz) - fz(vy)
                hy = fz(vx) - (nz - vz)
                hz = (ny - vy) - fy(vx)
                gy, gz = h_ref[2 * ch], h_ref[2 * ch + 1]
                h_ref[2 * ch] = hy
                h_ref[2 * ch + 1] = hz
                cx = by(hz) - bz(hy)
                cy = bz(hx) - (hz - gz)
                cz = (hy - gy) - by(hx)
                for comp, cv in enumerate((cx, cy, cz)):
                    o = e_ref[0, f, 1 - part, comp, p]
                    r_ref[3 * ch + comp, p] = cv + rotate_add(part, w, o) - s_ref[0, f, part, comp, p]
        return carry

    lax.fori_loop(0, PL, first, 0)
    for i in range(8):
        h_ref[i] = zero

    def second(p, carry):
        sig = c_ref[0, p]
        acc = zero
        for f in range(NF):
            om = om_ref[f]
            tot = zero
            dia = zero
            for part in range(2):
                ch = 2 * f + part
                vx, vy, vz = (r_ref[3 * ch + c, p] for c in range(3))
                ny = r_ref[3 * ch + 1, p + 1]
                nz = r_ref[3 * ch + 2, p + 1]
                hx = fy(vz) - fz(vy)
                hy = fz(vx) - (nz - vz)
                hz = (ny - vy) - fy(vx)
                gy, gz = h_ref[2 * ch], h_ref[2 * ch + 1]
                h_ref[2 * ch] = hy
                h_ref[2 * ch + 1] = hz
                cx = by(hz) - bz(hy)
                cy = bz(hx) - (hz - gz)
                cz = (hy - gy) - by(hx)
                o = [e_ref[0, f, 1 - part, c, p] for c in range(3)]
                s = [e_ref[0, f, part, c, p] for c in range(3)]
                t = o[0] * cx + o[1] * cy + o[2] * cz
                tot = tot + t if part == 1 else tot - t
                dia = dia + (s[0] * vx + s[1] * vy + s[2] * vz)
            acc = acc + (SCALE * om * live) * (tot + (om * sig) * dia)
        loc_ref[pl.ds(pl.multiple_of(p * NY, NY), NY), :] = acc
        return carry

    lax.fori_loop(0, PL, second, 0)

    bt = lax.broadcasted_iota(I32, (DEV, ROWS), 0) == rb_ref[...]
    hot = one_hot(bt)
    before = one_hot(lax.broadcasted_iota(I32, (ROWS, ROWS), 0) < lax.broadcasted_iota(I32, (ROWS, ROWS), 1))
    counts = dot(hot, before)
    rank = jnp.sum(jnp.where(bt, counts, 0.0), axis=0, keepdims=True)
    own8 = jnp.broadcast_to(own_ref[...].astype(F32), (8, DEV)).astype(BF16)
    dest = dot(own8, hot)[0:1]
    base = (dest * SLOTS).astype(I32)
    rank = rank.astype(I32)
    slot = base + rank
    slot_ref[...] = jnp.broadcast_to(slot, (8, ROWS))
    at = lax.broadcasted_iota(I32, (DEV * SLOTS, ROWS), 0)
    codes = jnp.where(lax.broadcasted_iota(I32, (NZ, ROWS), 0) == rank, (ro_ref[...] + 1).astype(F32), 0.0).astype(BF16)
    index = lax.dot_general(one_hot(at == base + CAP), codes, (((1,), (1,)), ((), ())), preferred_element_type=F32)
    out_ref[...] = index + exact_dot(one_hot(at == slot), loc_ref[...])


def finish_kernel(om_ref, tb_ref, elo_ref, ehi_ref, clo_ref, chi_ref, ups_ref, dns_ref, upr_ref, dnr_ref, slot_ref, part_ref, out_ref, loc_ref):
    brick, span = active_of(tb_ref)
    live = jnp.where(brick < span, 1.0, 0.0).astype(F32)
    low = jnp.where(brick > 0, 1.0, 0.0).astype(F32)
    nxt = jnp.where(brick + 1 < span, 1.0, 0.0).astype(F32)
    zero = jnp.zeros((NY, NZ), F32)
    acc = [zero, zero, zero, zero]
    for f in range(NF):
        om = om_ref[f]
        weight = SCALE * om * live
        tot = [zero, zero, zero, zero]
        dia = [zero, zero]
        for part in range(2):
            ch = 2 * f + part
            y, z = 2 * ch, 2 * ch + 1

            def add(which, terms):
                tot[which] = tot[which] + terms if part == 1 else tot[which] - terms

            ey, ez = dns_ref[y], dns_ref[z]
            dry = low * (ey - upr_ref[z])
            drz = low * (ez - upr_ref[y])
            ry, rz = dns_ref[8 + y] + dry, dns_ref[8 + z] + drz
            div = by(ey) + bz(ez)
            qy = upr_ref[8 + y] + fz(div) - ez
            qz = upr_ref[8 + z] + fy(div) - ey
            gy = low * (qy - rz)
            gz = low * (ry - qz)
            hx = fy(drz) - fz(dry)
            ax = -(by(dry) + bz(drz))
            ay = bz(hx) + dry + gz
            az = drz - by(hx) - gy
            o = [elo_ref[0, f, 1 - part, c, 0] for c in range(3)]
            add(0, o[0] * ax + o[1] * ay + o[2] * az)
            dia[0] = dia[0] + (ey * dry + ez * drz)
            add(1, -(elo_ref[0, f, 1 - part, 1, 1] * dry + elo_ref[0, f, 1 - part, 2, 1] * drz))

            ey, ez = nxt * dnr_ref[y], nxt * dnr_ref[z]
            dx = by(ey) + bz(ez)
            ry = nxt * (dnr_ref[8 + y] + (ey - ups_ref[z]))
            rz = nxt * (dnr_ref[8 + z] - (ups_ref[y] - ez))
            hx = fz(ey) - fy(ez)
            hy = fz(dx) - (rz + ez)
            hz = (ry + ey) - fy(dx)
            ax = by(hz) - bz(hy)
            ay = bz(hx) - (hz + ey)
            az = (hy - ez) - by(hx)
            o = [ehi_ref[0, f, 1 - part, c, 1] for c in range(3)]
            s = [ehi_ref[0, f, part, c, 1] for c in range(3)]
            add(3, o[0] * ax + o[1] * ay + o[2] * az)
            dia[1] = dia[1] + (s[0] * dx - s[1] * ey - s[2] * ez)
            o = [ehi_ref[0, f, 1 - part, c, 0] for c in range(3)]
            add(2, o[1] * ey + o[2] * ez - o[0] * dx)
        acc[0] = acc[0] + weight * (tot[0] + (om * clo_ref[0, 0]) * dia[0])
        acc[1] = acc[1] + weight * tot[1]
        acc[2] = acc[2] + weight * tot[2]
        acc[3] = acc[3] + weight * (tot[3] + (om * chi_ref[0, 0]) * dia[1])
    for i in range(4):
        loc_ref[i * NY:(i + 1) * NY, :] = acc[i]
    at = lax.broadcasted_iota(I32, (DEV * SLOTS, 2 * NY), 0)
    hot = jnp.concatenate(
        [one_hot(at == slot_ref[0:1, 0:2 * NY]), one_hot(at == slot_ref[0:1, ROWS - 2 * NY:ROWS])], axis=1
    )
    out_ref[...] = part_ref[...] + exact_dot(hot, loc_ref[...])


def owner_kernel(got_ref, out_ref):
    codes = got_ref[pl.ds(CAP, DEV, stride=SLOTS), :]
    offs = codes.T[0:CAP].astype(I32)
    want = lax.broadcasted_iota(I32, (G_DEV, DEV), 0) + 1
    total = jnp.zeros((G_DEV, NZ), F32)
    for k in range(CAP):
        hot = one_hot(want == offs[k:k + 1])
        total = total + exact_dot(hot, got_ref[pl.ds(k, DEV, stride=SLOTS), :])
    out_ref[...] = total


SMEM = pl.BlockSpec(memory_space=pltpu.SMEM)
LIMIT = 48 * 1024 * 1024


def full(shape):
    return pl.BlockSpec(shape, lambda i: (0,) * len(shape))


def planes(start, count):
    return pl.BlockSpec((1, NF, 2, 3, count, NY, NZ), lambda i: (0, 0, 0, 0, start // count, 0, 0))


def cells(start):
    return pl.BlockSpec((1, 1, NY, NZ), lambda i: (0, start, 0, 0))


def params():
    return pltpu.CompilerParams(vmem_limit_bytes=LIMIT)


def per_device(fields, sources, conductivity, omegas, tx_bricks, owner_map, row_brick, row_offset):
    pay = jax.ShapeDtypeStruct((16, NY, NZ), F32)
    up, dn = pl.pallas_call(
        payload_kernel,
        grid=(1,),
        in_specs=[SMEM, planes(0, 2), planes(6, 2), planes(0, 1), planes(7, 1), cells(0), cells(7)],
        out_specs=[full((16, NY, NZ))] * 2,
        out_shape=[pay, pay],
        compiler_params=params(),
        cost_estimate=pl.CostEstimate(flops=2_000_000, bytes_accessed=3_400_000, transcendentals=0),
        name="payload",
    )(omegas, fields, fields, sources, sources, conductivity, conductivity)
    ring = [(i, (i + 1) % BRICK) for i in range(BRICK)]
    back = [(b, a) for a, b in ring]
    up_got = lax.ppermute(up, "brick", ring)
    dn_got = lax.ppermute(dn, "brick", back)
    part, slot = pl.pallas_call(
        main_kernel,
        grid=(1,),
        in_specs=[
            SMEM,
            SMEM,
            full((1, NF, 2, 3, PL, NY, NZ)),
            full((1, NF, 2, 3, PL, NY, NZ)),
            full((1, PL, NY, NZ)),
            full((1, ROWS)),
            full((1, ROWS)),
            full((1, DEV)),
        ],
        out_specs=[full((DEV * SLOTS, NZ)), full((8, ROWS))],
        out_shape=[
            jax.ShapeDtypeStruct((DEV * SLOTS, NZ), F32),
            jax.ShapeDtypeStruct((8, ROWS), I32),
        ],
        scratch_shapes=[
            pltpu.VMEM((12, PL + 1, NY, NZ), F32),
            pltpu.VMEM((8, NY, NZ), F32),
            pltpu.VMEM((ROWS, NZ), F32),
        ],
        compiler_params=params(),
        cost_estimate=pl.CostEstimate(flops=60_000_000, bytes_accessed=8_000_000, transcendentals=0),
        name="interior",
    )(
        omegas,
        tx_bricks,
        fields,
        sources,
        conductivity,
        row_brick.reshape(1, ROWS),
        row_offset,
        owner_map.reshape(1, DEV),
    )
    packed = pl.pallas_call(
        finish_kernel,
        grid=(1,),
        in_specs=[SMEM, SMEM, planes(0, 2), planes(6, 2), cells(0), cells(7)]
        + [full((16, NY, NZ))] * 4
        + [full((8, ROWS)), full((DEV * SLOTS, NZ))],
        out_specs=full((DEV * SLOTS, NZ)),
        out_shape=jax.ShapeDtypeStruct((DEV * SLOTS, NZ), F32),
        scratch_shapes=[pltpu.VMEM((4 * NY, NZ), F32)],
        compiler_params=params(),
        cost_estimate=pl.CostEstimate(flops=40_000_000, bytes_accessed=4_000_000, transcendentals=0),
        name="finish",
    )(omegas, tx_bricks, fields, fields, conductivity, conductivity, up, dn, up_got, dn_got, slot, part)
    got = lax.all_to_all(
        packed.reshape(DEV, 1, SLOTS * NZ), ("tx", "brick"), 0, 0, tiled=True
    ).reshape(DEV * SLOTS, NZ)
    return pl.pallas_call(
        owner_kernel,
        grid=(1,),
        in_specs=[full((DEV * SLOTS, NZ))],
        out_specs=full((G_DEV, NZ)),
        out_shape=jax.ShapeDtypeStruct((G_DEV, NZ), F32),
        compiler_params=params(),
        name="owner_sum",
    )(got)


def solution(mesh):
    return jax.shard_map(
        per_device,
        mesh=mesh,
        in_specs=(
            P("tx", None, None, None, "brick", None, None),
            P("tx", None, None, None, "brick", None, None),
            P("tx", "brick", None, None),
            P(),
            P(),
            P(),
            P("tx", "brick", None),
            P("tx", "brick"),
        ),
        out_specs=P(("tx", "brick"), None),
        check_vma=False,
    )
```

```python
import jax
import jax.numpy as jnp
from jax import lax
from jax.experimental import pallas as pl
from jax.experimental.pallas import tpu as pltpu
from jax.sharding import PartitionSpec as P

PL, NY, NZ, NF = 8, 64, 128, 2
ROWS = PL * NY
G_DEV = 32
CAP = 8
DEV = 128
SLOTS = CAP + 1
BRICK = 16
PAD = 8
CH = 32
F32, BF16, I32 = jnp.float32, jnp.bfloat16, jnp.int32
SCALE = 0.003


def fy(v):
    rows = lax.broadcasted_iota(I32, v.shape, 0)
    return jnp.where(rows == NY - 1, 0.0, pltpu.roll(v, NY - 1, 0)) - v


def by(v):
    rows = lax.broadcasted_iota(I32, v.shape, 0)
    return v - jnp.where(rows == 0, 0.0, pltpu.roll(v, 1, 0))


def fz(v):
    lanes = lax.broadcasted_iota(I32, v.shape, 1)
    return jnp.where(lanes == NZ - 1, 0.0, pltpu.roll(v, NZ - 1, 1)) - v


def bz(v):
    lanes = lax.broadcasted_iota(I32, v.shape, 1)
    return v - jnp.where(lanes == 0, 0.0, pltpu.roll(v, 1, 1))


def q_of(vx, vy, vz):
    return fz(vx) + vz, vy + fy(vx)


def rotate(curl, part, weight, other):
    return curl - weight * other if part == 0 else curl + weight * other


def signed(part, value):
    return value if part == 1 else -value


def halo_kernel(
    om_hbm, e_hbm, s_hbm, c_hbm, up_ref, dn_ref, upr_ref, dnr_ref,
    om_ref, elo_ref, ehi_ref, slo_ref, shi_ref, cc_ref, sems,
):
    small = [
        pltpu.make_async_copy(om_hbm, om_ref, sems.at[8]),
        pltpu.make_async_copy(c_hbm.at[0, 0], cc_ref.at[0], sems.at[9]),
        pltpu.make_async_copy(c_hbm.at[0, PL - 1], cc_ref.at[1], sems.at[10]),
    ]
    big = [
        [
            pltpu.make_async_copy(e_hbm.at[0, f, :, :, pl.ds(PL - 2, 2)], ehi_ref.at[f], sems.at[4 * f]),
            pltpu.make_async_copy(s_hbm.at[0, f, :, :, PL - 1], shi_ref.at[f], sems.at[4 * f + 1]),
            pltpu.make_async_copy(e_hbm.at[0, f, :, :, pl.ds(0, 2)], elo_ref.at[f], sems.at[4 * f + 2]),
            pltpu.make_async_copy(s_hbm.at[0, f, :, pl.ds(1, 2), 0], slo_ref.at[f], sems.at[4 * f + 3]),
        ]
        for f in range(NF)
    ]
    for copy in small + big[0] + big[1]:
        copy.start()
    for copy in small:
        copy.wait()
    for f in range(NF):
        om = om_ref[f]
        big[f][0].wait()
        big[f][1].wait()
        for part in range(2):
            ch = 2 * f + part
            ux, uy, uz = (ehi_ref[f, part, c, 0] for c in range(3))
            vx, vy, vz = (ehi_ref[f, part, c, 1] for c in range(3))
            hy, qz = q_of(vx, vy, vz)
            up_ref[2 * ch] = hy
            up_ref[2 * ch + 1] = qz
            hz = -qz
            hx = fy(vz) - fz(vy)
            gy = fz(ux) - (vz - uz)
            gz = (vy - uy) - fy(ux)
            w = om * cc_ref[1]
            o = [ehi_ref[f, 1 - part, c, 1] for c in range(3)]
            rx = rotate(by(hz) - bz(hy), part, w, o[0]) - shi_ref[f, part, 0]
            ry = rotate(bz(hx) - (hz - gz), part, w, o[1]) - shi_ref[f, part, 1]
            rz = rotate((hy - gy) - by(hx), part, w, o[2]) - shi_ref[f, part, 2]
            sy, sz = q_of(rx, ry, rz)
            upr_ref[2 * ch] = sy
            upr_ref[2 * ch + 1] = sz
        big[f][2].wait()
        big[f][3].wait()
        for part in range(2):
            ch = 2 * f + part
            vx, vy, vz = (elo_ref[f, part, c, 0] for c in range(3))
            dn_ref[2 * ch] = vy
            dn_ref[2 * ch + 1] = vz
            hx = fy(vz) - fz(vy)
            hy = fz(vx) - (elo_ref[f, part, 2, 1] - vz)
            hz = (elo_ref[f, part, 1, 1] - vy) - fy(vx)
            w = om * cc_ref[0]
            dnr_ref[2 * ch] = rotate(bz(hx) - hz, part, w, elo_ref[f, 1 - part, 1, 0]) - slo_ref[f, part, 0]
            dnr_ref[2 * ch + 1] = rotate(hy - by(hx), part, w, elo_ref[f, 1 - part, 2, 0]) - slo_ref[f, part, 1]


def one_hot(cond):
    return jnp.where(cond, 1.0, 0.0).astype(BF16)


def dot(a, b):
    return jnp.dot(a, b, preferred_element_type=F32)


def pick(hot, v):
    hi = v.astype(BF16)
    low = (v - hi.astype(F32)).astype(BF16)
    both = dot(hot, jnp.concatenate([hi, low], axis=1))
    return both[:, 0:NZ] + both[:, NZ:2 * NZ]


def place(tb_ref):
    brick = lax.axis_index("brick")
    span = tb_ref[lax.axis_index("tx")]
    live = jnp.where(brick < span, 1.0, 0.0).astype(F32)
    low = jnp.where(brick > 0, 1.0, 0.0).astype(F32)
    nxt = jnp.where(brick + 1 < span, 1.0, 0.0).astype(F32)
    return live, low, nxt


EDGE = (0, 1, PL - 2, PL - 1)


def main_kernel(
    om_ref, tb_ref, e_hbm, s_hbm, c_hbm, rb_ref, ro_ref, own_ref,
    part_ref, slot_ref, loc_ref, edge_ref, sig_ref, own_r_ref,
    e_ref, s_ref, c_ref, r_ref, h_ref, g_ref, sems,
):
    cp = pltpu.make_async_copy(c_hbm.at[0], c_ref, sems.at[2 * PL])
    cp.start()

    def fetch_e(p):
        return pltpu.make_async_copy(e_hbm.at[0, :, :, :, p], e_ref.at[:, :, :, p, pl.ds(0, NY)], sems.at[p])

    def fetch_s(p):
        return pltpu.make_async_copy(s_hbm.at[0, :, :, :, p], s_ref.at[:, :, :, p], sems.at[PL + p])

    for p in range(PL):
        fetch_e(p).start()
        fetch_s(p).start()

    live, _, _ = place(tb_ref)
    zero = jnp.zeros((NY, NZ), F32)
    zpad = jnp.zeros((PAD, NZ), F32)
    for f in range(NF):
        for part in range(2):
            for c in range(3):
                i = 3 * (2 * f + part) + c
                r_ref[i, PL, 0:NY] = zero
                e_ref[f, part, c, PL, 0:NY] = zero
                for p in range(PL):
                    r_ref[i, p, NY:NY + PAD] = zpad
                    e_ref[f, part, c, p, NY:NY + PAD] = zpad
    for i in range(8):
        h_ref[i, 0:PAD] = zpad
        h_ref[i, PAD:PAD + NY] = zero
    for i in range(4):
        g_ref[i] = zero

    bt = lax.broadcasted_iota(I32, (DEV, ROWS), 0) == rb_ref[...]
    hot = one_hot(bt)
    before = one_hot(lax.broadcasted_iota(I32, (ROWS, ROWS), 0) < lax.broadcasted_iota(I32, (ROWS, ROWS), 1))
    counts = dot(hot, before)
    rank = jnp.sum(jnp.where(bt, counts, 0.0), axis=0, keepdims=True)
    own8 = jnp.broadcast_to(own_ref[...].astype(F32), (8, DEV)).astype(BF16)
    dest = dot(own8, hot)[0:1].astype(I32)
    rank = rank.astype(I32)
    slot = dest * SLOTS + rank
    slot_ref[...] = jnp.broadcast_to(slot, (8, ROWS))
    codes = jnp.where(lax.broadcasted_iota(I32, (NZ, ROWS), 0) == rank, (ro_ref[...] + 1).astype(F32), 0.0).astype(BF16)
    mine = one_hot(lax.broadcasted_iota(I32, (DEV, ROWS), 0) == dest)
    index = lax.dot_general(mine, codes, (((1,), (1,)), ((), ())), preferred_element_type=F32)

    def curl(get, at, p, y, ch):
        lanes = lax.broadcasted_iota(I32, (CH, NZ), 1)

        def nz_(v):
            return jnp.where(lanes == NZ - 1, 0.0, pltpu.roll(v, NZ - 1, 1))

        def pz_(v):
            return jnp.where(lanes == 0, 0.0, pltpu.roll(v, 1, 1))

        vx, vy, vz = (get(c, p, y) for c in range(3))
        hx = (get(2, p, y + 1) - vz) - (nz_(vy) - vy)
        hy = (nz_(vx) - vx) - (get(2, p + 1, y) - vz)
        hz = (get(1, p + 1, y) - vy) - (get(0, p, y + 1) - vx)
        gy = g_ref[ch, y:y + CH]
        gz = h_ref[2 * ch + 1, PAD + y:PAD + y + CH]
        h_ref[2 * ch, PAD + y:PAD + y + CH] = hx
        h_ref[2 * ch + 1, PAD + y:PAD + y + CH] = hz
        g_ref[ch, y:y + CH] = hy
        hxp = h_ref[2 * ch, PAD + y - 1:PAD + y - 1 + CH]
        hzp = h_ref[2 * ch + 1, PAD + y - 1:PAD + y - 1 + CH]
        cx = (hz - hzp) - (hy - pz_(hy))
        cy = (hx - pz_(hx)) - (hz - gz)
        cz = (hy - gy) - (hx - hxp)
        return (vx, vy, vz), (cx, cy, cz)

    cp.wait()
    fetch_e(0).wait()

    def first(p, carry):
        @pl.when(p < PL - 1)
        def _():
            fetch_e(p + 1).wait()

        fetch_s(p).wait()
        for y in range(0, NY, CH):
            sig = c_ref[p, y:y + CH]
            for f in range(NF):
                w = om_ref[f] * sig
                for part in range(2):
                    _, cs = curl(lambda c, q, r: e_ref[f, part, c, q, r:r + CH], 0, p, y, 2 * f + part)
                    for c in range(3):
                        o = e_ref[f, 1 - part, c, p, y:y + CH]
                        r_ref[3 * (2 * f + part) + c, p, y:y + CH] = rotate(cs[c], part, w, o) - s_ref[f, part, c, p, y:y + CH]
        return carry

    lax.fori_loop(0, PL, first, 0)
    for i in range(4):
        h_ref[2 * i + 1, PAD:PAD + NY] = zero
        g_ref[i] = zero

    def second(p, carry):
        for y in range(0, NY, CH):
            sig = c_ref[p, y:y + CH]
            acc = jnp.zeros((CH, NZ), F32)
            for f in range(NF):
                om = om_ref[f]
                tot = jnp.zeros((CH, NZ), F32)
                dia = jnp.zeros((CH, NZ), F32)
                for part in range(2):
                    ch = 2 * f + part
                    vs, cs = curl(lambda c, q, r: r_ref[3 * ch + c, q, r:r + CH], 0, p, y, ch)
                    o = [e_ref[f, 1 - part, c, p, y:y + CH] for c in range(3)]
                    s = [e_ref[f, part, c, p, y:y + CH] for c in range(3)]
                    tot = tot + signed(part, o[0] * cs[0] + o[1] * cs[1] + o[2] * cs[2])
                    dia = dia + (s[0] * vs[0] + s[1] * vs[1] + s[2] * vs[2])
                acc = acc + (SCALE * om * live) * (tot + (om * sig) * dia)
            loc_ref[pl.ds(pl.multiple_of(p * NY + y, CH), CH), :] = acc
        return carry

    lax.fori_loop(0, PL, second, 0)

    for f in range(NF):
        for part in range(2):
            for c in range(3):
                for i, p in enumerate(EDGE):
                    edge_ref[3 * (2 * f + part) + c, i] = e_ref[f, part, c, p, 0:NY]
    for ch in range(4):
        own_r_ref[2 * ch] = r_ref[3 * ch + 1, 0, 0:NY]
        own_r_ref[2 * ch + 1] = r_ref[3 * ch + 2, 0, 0:NY]
    sig_ref[0] = c_ref[0]
    sig_ref[1] = c_ref[PL - 1]
    lo, hi = 2 * NY, ROWS - 2 * NY
    at = lax.broadcasted_iota(I32, (DEV * SLOTS, hi - lo), 0)
    part_ref[...] = pick(one_hot(at == slot[:, lo:hi]), loc_ref[lo:hi])
    part_ref[pl.ds(CAP, DEV, stride=SLOTS), :] = index


def field_fix_kernel(
    om_ref, tb_ref, edge_ref, sig_ref, loc_ref, ups_ref, dns_ref, dnr_ref, upg_ref, dng_ref, slot_ref, part_ref,
    out_ref, rest_ref, fac_ref, two_ref,
):
    live, low, nxt = place(tb_ref)
    zero = jnp.zeros((NY, NZ), F32)
    acc = [zero] * 4
    for f in range(NF):
        om = om_ref[f]
        weight = SCALE * om * live
        tot = [zero] * 4
        dia = [zero, zero]
        for part in range(2):
            ch = 2 * f + part
            mine, other = 3 * ch, 3 * (2 * f + 1 - part)
            y, z = 2 * ch, 2 * ch + 1

            def add(which, terms):
                tot[which] = tot[which] + signed(part, terms)

            ey, ez = dns_ref[y], dns_ref[z]
            dry = low * (ey - upg_ref[z])
            drz = low * (ez - upg_ref[y])
            ry, rz = dnr_ref[y] + dry, dnr_ref[z] + drz
            div = by(ey) + bz(ez)
            gy = low * (fz(div) - ez - rz)
            gz = low * (ry - fy(div) + ey)
            hx = fy(drz) - fz(dry)
            ax = -(by(dry) + bz(drz))
            ay = bz(hx) + dry + gz
            az = drz - by(hx) - gy
            o = [edge_ref[other + c, 0] for c in range(3)]
            add(0, o[0] * ax + o[1] * ay + o[2] * az)
            dia[0] = dia[0] + (ey * dry + ez * drz)
            add(1, -(edge_ref[other + 1, 1] * dry + edge_ref[other + 2, 1] * drz))
            scale = signed(part, weight) * low
            fac_ref[2 * ch] = -scale * o[2]
            fac_ref[2 * ch + 1] = -scale * o[1]

            ey, ez = nxt * dng_ref[y], nxt * dng_ref[z]
            dx = by(ey) + bz(ez)
            ry = nxt * (ey - ups_ref[z])
            rz = nxt * (ez - ups_ref[y])
            hx = fz(ey) - fy(ez)
            hy = fz(dx) - (rz + ez)
            hz = (ry + ey) - fy(dx)
            ax = by(hz) - bz(hy)
            ay = bz(hx) - (hz + ey)
            az = (hy - ez) - by(hx)
            o = [edge_ref[other + c, 3] for c in range(3)]
            s = [edge_ref[mine + c, 3] for c in range(3)]
            add(3, o[0] * ax + o[1] * ay + o[2] * az)
            dia[1] = dia[1] + (s[0] * dx - s[1] * ey - s[2] * ez)
            scale = signed(part, weight) * nxt
            for c in range(3):
                fac_ref[8 + 3 * ch + c] = scale * o[c]
            o = [edge_ref[other + c, 2] for c in range(3)]
            add(2, o[1] * ey + o[2] * ez - o[0] * dx)
        acc[0] = acc[0] + weight * (tot[0] + (om * sig_ref[0]) * dia[0])
        acc[1] = acc[1] + weight * tot[1]
        acc[2] = acc[2] + weight * tot[2]
        acc[3] = acc[3] + weight * (tot[3] + (om * sig_ref[1]) * dia[1])
    rest_ref[0] = loc_ref[0:NY] + acc[0]
    rest_ref[1] = loc_ref[ROWS - NY:ROWS] + acc[3]
    two_ref[0:NY] = loc_ref[NY:2 * NY] + acc[1]
    two_ref[NY:2 * NY] = loc_ref[ROWS - 2 * NY:ROWS - NY] + acc[2]
    at = lax.broadcasted_iota(I32, (DEV * SLOTS, NY), 0)
    hot = jnp.concatenate(
        [one_hot(at == slot_ref[0:1, NY:2 * NY]), one_hot(at == slot_ref[0:1, ROWS - 2 * NY:ROWS - NY])], axis=1
    )
    out_ref[...] = part_ref[...] + pick(hot, two_ref[...])


def residual_fix_kernel(fac_ref, rest_ref, upg_ref, dng_ref, slot_ref, part_ref, out_ref, two_ref):
    low, high = rest_ref[0], rest_ref[1]
    for ch in range(4):
        low = low + (fac_ref[2 * ch] * upg_ref[2 * ch] + fac_ref[2 * ch + 1] * upg_ref[2 * ch + 1])
        ry, rz = dng_ref[2 * ch], dng_ref[2 * ch + 1]
        o = [fac_ref[8 + 3 * ch + c] for c in range(3)]
        high = high + (o[0] * (by(ry) + bz(rz)) - o[1] * ry - o[2] * rz)
    two_ref[0:NY] = low
    two_ref[NY:2 * NY] = high
    at = lax.broadcasted_iota(I32, (DEV * SLOTS, NY), 0)
    hot = jnp.concatenate([one_hot(at == slot_ref[0:1, 0:NY]), one_hot(at == slot_ref[0:1, ROWS - NY:ROWS])], axis=1)
    out_ref[...] = part_ref[...] + pick(hot, two_ref[...])


def owner_kernel(got_ref, out_ref):
    codes = got_ref[pl.ds(CAP, DEV, stride=SLOTS), :]
    offs = codes.T[0:CAP].astype(I32)
    want = lax.broadcasted_iota(I32, (G_DEV, DEV), 0) + 1
    total = jnp.zeros((G_DEV, NZ), F32)
    for k in range(CAP):
        total = total + pick(one_hot(want == offs[k:k + 1]), got_ref[pl.ds(k, DEV, stride=SLOTS), :])
    out_ref[...] = total


SMEM = pl.BlockSpec(memory_space=pltpu.SMEM)
VMEM = pl.BlockSpec(memory_space=pltpu.VMEM)
HBM = pl.BlockSpec(memory_space=pltpu.HBM)
LIMIT = 40 * 1024 * 1024


def f32(*shape):
    return jax.ShapeDtypeStruct(shape, F32)


def call(kernel, name, ins, outs, scratch, flops, moved):
    return pl.pallas_call(
        kernel,
        in_specs=ins,
        out_specs=[VMEM] * len(outs),
        out_shape=outs,
        scratch_shapes=scratch,
        compiler_params=pltpu.CompilerParams(vmem_limit_bytes=LIMIT),
        cost_estimate=pl.CostEstimate(flops=flops, bytes_accessed=moved, transcendentals=0),
        name=name,
    )


def per_device(fields, sources, conductivity, omegas, tx_bricks, owner_map, row_brick, row_offset):
    omegas_in = omegas
    fields, sources, conductivity, omegas = (
        pltpu.with_memory_space_constraint(x, pltpu.HBM) for x in (fields, sources, conductivity, omegas)
    )
    ring = [(i, (i + 1) % BRICK) for i in range(BRICK)]
    back = [(b, a) for a, b in ring]
    pay = f32(8, NY, NZ)
    packed = f32(DEV * SLOTS, NZ)
    dma = pltpu.SemaphoreType.DMA
    up_e, dn_e, up_r, dn_r = call(
        halo_kernel, "halo", [HBM] * 4, [pay] * 4,
        [
            pltpu.SMEM((NF,), F32),
            pltpu.VMEM((NF, 2, 3, 2, NY, NZ), F32),
            pltpu.VMEM((NF, 2, 3, 2, NY, NZ), F32),
            pltpu.VMEM((NF, 2, 2, NY, NZ), F32),
            pltpu.VMEM((NF, 2, 3, NY, NZ), F32),
            pltpu.VMEM((2, NY, NZ), F32),
            dma((11,)),
        ], 2_000_000, 3_000_000,
    )(omegas, fields, sources, conductivity)
    upg_e = lax.ppermute(up_e, "brick", ring)
    dng_e = lax.ppermute(dn_e, "brick", back)
    upg_r = lax.ppermute(up_r, "brick", ring)
    dng_r = lax.ppermute(dn_r, "brick", back)
    part, slot, loc, edge, sig, own_r = call(
        main_kernel, "interior", [SMEM, SMEM, HBM, HBM, HBM, VMEM, VMEM, VMEM],
        [packed, jax.ShapeDtypeStruct((8, ROWS), I32), f32(ROWS, NZ), f32(12, 4, NY, NZ), f32(2, NY, NZ), pay],
        [
            pltpu.VMEM((NF, 2, 3, PL + 1, NY + PAD, NZ), F32),
            pltpu.VMEM((NF, 2, 3, PL, NY, NZ), F32),
            pltpu.VMEM((PL, NY, NZ), F32),
            pltpu.VMEM((12, PL + 1, NY + PAD, NZ), F32),
            pltpu.VMEM((8, PAD + NY, NZ), F32),
            pltpu.VMEM((4, NY, NZ), F32),
            dma((2 * PL + 1,)),
        ], 60_000_000, 8_000_000,
    )(
        omegas_in, tx_bricks, fields, sources, conductivity,
        row_brick.reshape(1, ROWS), row_offset, owner_map.reshape(1, DEV),
    )
    part, rest, fac = call(
        field_fix_kernel, "field_fix", [SMEM, SMEM] + [VMEM] * 10,
        [packed, f32(2, NY, NZ), f32(20, NY, NZ)], [pltpu.VMEM((2 * NY, NZ), F32)], 20_000_000, 4_000_000,
    )(omegas_in, tx_bricks, edge, sig, loc, up_e, dn_e, own_r, upg_e, dng_e, slot, part)
    (send,) = call(
        residual_fix_kernel, "residual_fix", [VMEM] * 6, [packed], [pltpu.VMEM((2 * NY, NZ), F32)], 20_000_000, 3_000_000,
    )(fac, rest, upg_r, dng_r, slot, part)
    got = lax.all_to_all(send.reshape(DEV, 1, SLOTS * NZ), ("tx", "brick"), 0, 0, tiled=True).reshape(DEV * SLOTS, NZ)
    return pl.pallas_call(
        owner_kernel,
        in_specs=[VMEM],
        out_specs=VMEM,
        out_shape=f32(G_DEV, NZ),
        compiler_params=pltpu.CompilerParams(vmem_limit_bytes=LIMIT),
        name="owner_sum",
    )(got)


def solution(mesh):
    return jax.shard_map(
        per_device,
        mesh=mesh,
        in_specs=(
            P("tx", None, None, None, "brick", None, None),
            P("tx", None, None, None, "brick", None, None),
            P("tx", "brick", None, None),
            P(),
            P(),
            P(),
            P("tx", "brick", None),
            P("tx", "brick"),
        ),
        out_specs=P(("tx", "brick"), None),
        check_vma=False,
    )
```

```python
import jax
import jax.numpy as jnp
from jax import lax
from jax.experimental import pallas as pl
from jax.experimental.pallas import tpu as pltpu
from jax.sharding import Mesh, PartitionSpec as P

PL, NY, NZ, NF = 8, 64, 128, 2
ROWS = PL * NY
G_DEV = 32
CAP = 8
DEV = 128
SLOTS = CAP + 1
BRICK = 16
TX_AXES, BRICK_AXES = ("y", "core"), ("x", "z")
SWAP_AXES = ("core", "x", "z", "y")
PAD = 8
CH = 16
F32, BF16, I32 = jnp.float32, jnp.bfloat16, jnp.int32
SCALE = 0.003


def fy(v):
    rows = lax.broadcasted_iota(I32, v.shape, 0)
    return jnp.where(rows == NY - 1, 0.0, pltpu.roll(v, NY - 1, 0)) - v


def by(v):
    rows = lax.broadcasted_iota(I32, v.shape, 0)
    return v - jnp.where(rows == 0, 0.0, pltpu.roll(v, 1, 0))


def fz(v):
    lanes = lax.broadcasted_iota(I32, v.shape, 1)
    return jnp.where(lanes == NZ - 1, 0.0, pltpu.roll(v, NZ - 1, 1)) - v


def bz(v):
    lanes = lax.broadcasted_iota(I32, v.shape, 1)
    return v - jnp.where(lanes == 0, 0.0, pltpu.roll(v, 1, 1))


def q_of(vx, vy, vz):
    return fz(vx) + vz, vy + fy(vx)


def rotate(curl, part, weight, other):
    return curl - weight * other if part == 0 else curl + weight * other


def signed(part, value):
    return value if part == 1 else -value


def odd_brick():
    return (lax.axis_index(BRICK_AXES) & 1) == 1


def field_halo_kernel(e_hbm, one_ref, two_ref, lo_ref, hi_ref, sems):
    odd = odd_brick()
    lo = [pltpu.make_async_copy(e_hbm.at[0, f, :, pl.ds(1, 2), 0], lo_ref.at[f], sems.at[f]) for f in range(NF)]
    hi = [pltpu.make_async_copy(e_hbm.at[0, f, :, :, PL - 1], hi_ref.at[f], sems.at[NF + f]) for f in range(NF)]
    for f in range(NF):
        hi[f].start()
        lo[f].start()
    for f in range(NF):
        hi[f].wait()
        lo[f].wait()
        for part in range(2):
            q = q_of(*(hi_ref[f, part, c] for c in range(3)))
            for c in range(2):
                at = 2 * (2 * f + part) + c
                one_ref[at] = jnp.where(odd, q[c], lo_ref[f, part, c])
                two_ref[at] = jnp.where(odd, lo_ref[f, part, c], q[c])


def residual_halo_kernel(om_hbm, e_hbm, s_hbm, c_hbm, one_ref, two_ref, om_ref, elo_ref, ehi_ref, slo_ref, shi_ref, cc_ref, sems):
    odd = odd_brick()
    small = [
        pltpu.make_async_copy(om_hbm, om_ref, sems.at[8]),
        pltpu.make_async_copy(c_hbm.at[0, 0], cc_ref.at[0], sems.at[9]),
        pltpu.make_async_copy(c_hbm.at[0, PL - 1], cc_ref.at[1], sems.at[10]),
    ]
    big = [
        [
            pltpu.make_async_copy(e_hbm.at[0, f, :, :, pl.ds(0, 2)], elo_ref.at[f], sems.at[4 * f]),
            pltpu.make_async_copy(s_hbm.at[0, f, :, pl.ds(1, 2), 0], slo_ref.at[f], sems.at[4 * f + 1]),
            pltpu.make_async_copy(e_hbm.at[0, f, :, :, pl.ds(PL - 2, 2)], ehi_ref.at[f], sems.at[4 * f + 2]),
            pltpu.make_async_copy(s_hbm.at[0, f, :, :, PL - 1], shi_ref.at[f], sems.at[4 * f + 3]),
        ]
        for f in range(NF)
    ]
    for copy in small + big[0] + big[1]:
        copy.start()
    for copy in small:
        copy.wait()
    for f in range(NF):
        for copy in big[f]:
            copy.wait()
        om = om_ref[f]
        for part in range(2):
            ch = 2 * f + part
            vx, vy, vz = (elo_ref[f, part, c, 0] for c in range(3))
            hx = fy(vz) - fz(vy)
            hy = fz(vx) - (elo_ref[f, part, 2, 1] - vz)
            hz = (elo_ref[f, part, 1, 1] - vy) - fy(vx)
            w = om * cc_ref[0]
            dy = rotate(bz(hx) - hz, part, w, elo_ref[f, 1 - part, 1, 0]) - slo_ref[f, part, 0]
            dz = rotate(hy - by(hx), part, w, elo_ref[f, 1 - part, 2, 0]) - slo_ref[f, part, 1]
            ux, uy, uz = (ehi_ref[f, part, c, 0] for c in range(3))
            vx, vy, vz = (ehi_ref[f, part, c, 1] for c in range(3))
            hy, qz = q_of(vx, vy, vz)
            hz = -qz
            hx = fy(vz) - fz(vy)
            gy = fz(ux) - (vz - uz)
            gz = (vy - uy) - fy(ux)
            w = om * cc_ref[1]
            o = [ehi_ref[f, 1 - part, c, 1] for c in range(3)]
            rx = rotate(by(hz) - bz(hy), part, w, o[0]) - shi_ref[f, part, 0]
            ry = rotate(bz(hx) - (hz - gz), part, w, o[1]) - shi_ref[f, part, 1]
            rz = rotate((hy - gy) - by(hx), part, w, o[2]) - shi_ref[f, part, 2]
            sy, sz = q_of(rx, ry, rz)
            one_ref[2 * ch] = jnp.where(odd, sy, dy)
            one_ref[2 * ch + 1] = jnp.where(odd, sz, dz)
            two_ref[2 * ch] = jnp.where(odd, dy, sy)
            two_ref[2 * ch + 1] = jnp.where(odd, dz, sz)


def one_hot(cond):
    return jnp.where(cond, 1.0, 0.0).astype(BF16)


def dot(a, b):
    return jnp.dot(a, b, preferred_element_type=F32)


def pick(hot, v):
    hi = v.astype(BF16)
    low = (v - hi.astype(F32)).astype(BF16)
    both = dot(hot, jnp.concatenate([hi, low], axis=1))
    return both[:, 0:NZ] + both[:, NZ:2 * NZ]


def place(tb_ref):
    brick = lax.axis_index(BRICK_AXES)
    span = tb_ref[lax.axis_index(TX_AXES)]
    live = jnp.where(brick < span, 1.0, 0.0).astype(F32)
    low = jnp.where(brick > 0, 1.0, 0.0).astype(F32)
    nxt = jnp.where(brick + 1 < span, 1.0, 0.0).astype(F32)
    return live, low, nxt


def main_kernel(
    om_ref, tb_ref, e_ref, s_ref, c_ref, rb_ref, ro_ref, own_ref,
    part_ref, slot_ref, loc_ref, own_r_ref,
    r_ref, h_ref, g_ref,
):
    live, _, _ = place(tb_ref)
    zero = jnp.zeros((NY, NZ), F32)
    zpad = jnp.zeros((PAD, NZ), F32)
    for i in range(12):
        r_ref[i, PL, 0:NY] = zero
        for p in range(PL):
            r_ref[i, p, NY:NY + PAD] = zpad
    for i in range(8):
        h_ref[i, 0:PAD] = zpad
        h_ref[i, PAD:PAD + NY] = zero
    for i in range(4):
        g_ref[i] = zero

    bt = lax.broadcasted_iota(I32, (DEV, ROWS), 0) == rb_ref[...]
    hot = one_hot(bt)
    before = one_hot(lax.broadcasted_iota(I32, (ROWS, ROWS), 0) < lax.broadcasted_iota(I32, (ROWS, ROWS), 1))
    counts = dot(hot, before)
    rank = jnp.sum(jnp.where(bt, counts, 0.0), axis=0, keepdims=True)
    own8 = jnp.broadcast_to(own_ref[...].astype(F32), (8, DEV)).astype(BF16)
    dest = dot(own8, hot)[0:1].astype(I32)
    dest = ((dest >> 4) & 1) * 64 + ((dest >> 2) & 3) * 16 + (dest & 3) * 4 + (dest >> 5)
    rank = rank.astype(I32)
    slot = dest * SLOTS + rank
    slot_ref[...] = jnp.broadcast_to(slot, (8, ROWS))
    codes = jnp.where(lax.broadcasted_iota(I32, (NZ, ROWS), 0) == rank, (ro_ref[...] + 1).astype(F32), 0.0).astype(BF16)
    mine = one_hot(lax.broadcasted_iota(I32, (DEV, ROWS), 0) == dest)
    index = lax.dot_general(mine, codes, (((1,), (1,)), ((), ())), preferred_element_type=F32)

    def curl(get, p, y, ch):
        lanes = lax.broadcasted_iota(I32, (CH, NZ), 1)

        def nz_(v):
            return jnp.where(lanes == NZ - 1, 0.0, pltpu.roll(v, NZ - 1, 1))

        def pz_(v):
            return jnp.where(lanes == 0, 0.0, pltpu.roll(v, 1, 1))

        vx, vy, vz = (get(c, p, y) for c in range(3))
        hx = (get(2, p, y + 1) - vz) - (nz_(vy) - vy)
        hy = (nz_(vx) - vx) - (get(2, p + 1, y) - vz)
        hz = (get(1, p + 1, y) - vy) - (get(0, p, y + 1) - vx)
        gy = g_ref[ch, y:y + CH]
        gz = h_ref[2 * ch + 1, PAD + y:PAD + y + CH]
        h_ref[2 * ch, PAD + y:PAD + y + CH] = hx
        h_ref[2 * ch + 1, PAD + y:PAD + y + CH] = hz
        g_ref[ch, y:y + CH] = hy
        hxp = h_ref[2 * ch, PAD + y - 1:PAD + y - 1 + CH]
        hzp = h_ref[2 * ch + 1, PAD + y - 1:PAD + y - 1 + CH]
        cx = (hz - hzp) - (hy - pz_(hy))
        cy = (hx - pz_(hx)) - (hz - gz)
        cz = (hy - gy) - (hx - hxp)
        return (vx, vy, vz), (cx, cy, cz)

    rows = lax.broadcasted_iota(I32, (CH, NZ), 0)

    def first(p, carry):
        after = jnp.minimum(p + 1, PL - 1)
        inside = jnp.where(p < PL - 1, 1.0, 0.0).astype(F32)
        for y in range(0, NY, CH):
            sig = c_ref[0, p, y:y + CH]
            for f in range(NF):
                w = om_ref[f] * sig
                for part in range(2):

                    def get(c, q, r):
                        if q is not p:
                            return e_ref[0, f, part, c, after, r:r + CH] * inside
                        if r + CH <= NY:
                            return e_ref[0, f, part, c, p, r:r + CH]
                        last = e_ref[0, f, part, c, p, NY - CH:NY]
                        return jnp.where(rows == CH - 1, 0.0, pltpu.roll(last, CH - 1, 0))

                    _, cs = curl(get, p, y, 2 * f + part)
                    for c in range(3):
                        o = e_ref[0, f, 1 - part, c, p, y:y + CH]
                        r_ref[3 * (2 * f + part) + c, p, y:y + CH] = rotate(cs[c], part, w, o) - s_ref[0, f, part, c, p, y:y + CH]
        return carry

    lax.fori_loop(0, PL, first, 0)
    for i in range(4):
        h_ref[2 * i + 1, PAD:PAD + NY] = zero
        g_ref[i] = zero

    def second(p, carry):
        for y in range(0, NY, CH):
            sig = c_ref[0, p, y:y + CH]
            acc = jnp.zeros((CH, NZ), F32)
            for f in range(NF):
                om = om_ref[f]
                tot = jnp.zeros((CH, NZ), F32)
                dia = jnp.zeros((CH, NZ), F32)
                for part in range(2):
                    ch = 2 * f + part
                    vs, cs = curl(lambda c, q, r: r_ref[3 * ch + c, q, r:r + CH], p, y, ch)
                    o = [e_ref[0, f, 1 - part, c, p, y:y + CH] for c in range(3)]
                    s = [e_ref[0, f, part, c, p, y:y + CH] for c in range(3)]
                    tot = tot + signed(part, o[0] * cs[0] + o[1] * cs[1] + o[2] * cs[2])
                    dia = dia + (s[0] * vs[0] + s[1] * vs[1] + s[2] * vs[2])
                acc = acc + (SCALE * om * live) * (tot + (om * sig) * dia)
            loc_ref[pl.ds(pl.multiple_of(p * NY + y, CH), CH), :] = acc
        return carry

    lax.fori_loop(0, PL, second, 0)

    for ch in range(4):
        own_r_ref[2 * ch] = r_ref[3 * ch + 1, 0, 0:NY]
        own_r_ref[2 * ch + 1] = r_ref[3 * ch + 2, 0, 0:NY]
    lo, hi = 2 * NY, ROWS - 2 * NY
    at = lax.broadcasted_iota(I32, (DEV * SLOTS, hi - lo), 0)
    part_ref[...] = pick(one_hot(at == slot[:, lo:hi]), loc_ref[lo:hi])
    part_ref[pl.ds(CAP, DEV, stride=SLOTS), :] = index


def field_fix_kernel(
    om_ref, tb_ref, e_ref, c_ref, loc_ref, one_ref, two_ref, dnr_ref, gone_ref, gtwo_ref, slot_ref, part_ref,
    out_ref, rest_ref, fac_ref, rows_ref,
):
    odd = odd_brick()
    live, low, nxt = place(tb_ref)
    zero = jnp.zeros((NY, NZ), F32)
    acc = [zero] * 4
    for f in range(NF):
        om = om_ref[f]
        weight = SCALE * om * live
        tot = [zero] * 4
        dia = [zero, zero]
        for part in range(2):
            ch = 2 * f + part
            y, z = 2 * ch, 2 * ch + 1

            def add(which, terms):
                tot[which] = tot[which] + signed(part, terms)

            ey, ez = e_ref[0, f, part, 1, 0], e_ref[0, f, part, 2, 0]
            qy = jnp.where(odd, gtwo_ref[y], gone_ref[y])
            qz = jnp.where(odd, gtwo_ref[z], gone_ref[z])
            dry = low * (ey - qz)
            drz = low * (ez - qy)
            ry, rz = dnr_ref[y] + dry, dnr_ref[z] + drz
            div = by(ey) + bz(ez)
            gy = low * (fz(div) - ez - rz)
            gz = low * (ry - fy(div) + ey)
            hx = fy(drz) - fz(dry)
            ax = -(by(dry) + bz(drz))
            ay = bz(hx) + dry + gz
            az = drz - by(hx) - gy
            o = [e_ref[0, f, 1 - part, c, 0] for c in range(3)]
            add(0, o[0] * ax + o[1] * ay + o[2] * az)
            dia[0] = dia[0] + (ey * dry + ez * drz)
            add(1, -(e_ref[0, f, 1 - part, 1, 1] * dry + e_ref[0, f, 1 - part, 2, 1] * drz))
            scale = signed(part, weight) * low
            fac_ref[2 * ch] = -scale * o[2]
            fac_ref[2 * ch + 1] = -scale * o[1]

            ey = nxt * jnp.where(odd, gone_ref[y], gtwo_ref[y])
            ez = nxt * jnp.where(odd, gone_ref[z], gtwo_ref[z])
            qy = jnp.where(odd, one_ref[y], two_ref[y])
            qz = jnp.where(odd, one_ref[z], two_ref[z])
            dx = by(ey) + bz(ez)
            ry = nxt * (ey - qz)
            rz = nxt * (ez - qy)
            hx = fz(ey) - fy(ez)
            hy = fz(dx) - (rz + ez)
            hz = (ry + ey) - fy(dx)
            ax = by(hz) - bz(hy)
            ay = bz(hx) - (hz + ey)
            az = (hy - ez) - by(hx)
            o = [e_ref[0, f, 1 - part, c, PL - 1] for c in range(3)]
            s = [e_ref[0, f, part, c, PL - 1] for c in range(3)]
            add(3, o[0] * ax + o[1] * ay + o[2] * az)
            dia[1] = dia[1] + (s[0] * dx - s[1] * ey - s[2] * ez)
            scale = signed(part, weight) * nxt
            for c in range(3):
                fac_ref[8 + 3 * ch + c] = scale * o[c]
            o = [e_ref[0, f, 1 - part, c, PL - 2] for c in range(3)]
            add(2, o[1] * ey + o[2] * ez - o[0] * dx)
        acc[0] = acc[0] + weight * (tot[0] + (om * c_ref[0, 0]) * dia[0])
        acc[1] = acc[1] + weight * tot[1]
        acc[2] = acc[2] + weight * tot[2]
        acc[3] = acc[3] + weight * (tot[3] + (om * c_ref[0, PL - 1]) * dia[1])
    rest_ref[0] = loc_ref[0:NY] + acc[0]
    rest_ref[1] = loc_ref[ROWS - NY:ROWS] + acc[3]
    rows_ref[0:NY] = loc_ref[NY:2 * NY] + acc[1]
    rows_ref[NY:2 * NY] = loc_ref[ROWS - 2 * NY:ROWS - NY] + acc[2]
    at = lax.broadcasted_iota(I32, (DEV * SLOTS, NY), 0)
    hot = jnp.concatenate(
        [one_hot(at == slot_ref[0:1, NY:2 * NY]), one_hot(at == slot_ref[0:1, ROWS - 2 * NY:ROWS - NY])], axis=1
    )
    out_ref[...] = part_ref[...] + pick(hot, rows_ref[...])


def residual_fix_kernel(fac_ref, rest_ref, gone_ref, gtwo_ref, slot_ref, part_ref, out_ref, two_ref):
    odd = odd_brick()
    low, high = rest_ref[0], rest_ref[1]
    for ch in range(4):
        first = [gone_ref[2 * ch + c] for c in range(2)]
        second = [gtwo_ref[2 * ch + c] for c in range(2)]
        qy, qz = (jnp.where(odd, second[c], first[c]) for c in range(2))
        ry, rz = (jnp.where(odd, first[c], second[c]) for c in range(2))
        low = low + (fac_ref[2 * ch] * qy + fac_ref[2 * ch + 1] * qz)
        o = [fac_ref[8 + 3 * ch + c] for c in range(3)]
        high = high + (o[0] * (by(ry) + bz(rz)) - o[1] * ry - o[2] * rz)
    two_ref[0:NY] = low
    two_ref[NY:2 * NY] = high
    at = lax.broadcasted_iota(I32, (DEV * SLOTS, NY), 0)
    hot = jnp.concatenate([one_hot(at == slot_ref[0:1, 0:NY]), one_hot(at == slot_ref[0:1, ROWS - NY:ROWS])], axis=1)
    out_ref[...] = part_ref[...] + pick(hot, two_ref[...])


def owner_kernel(got_ref, out_ref):
    codes = got_ref[pl.ds(CAP, DEV, stride=SLOTS), :]
    offs = codes.T[0:CAP].astype(I32)
    want = lax.broadcasted_iota(I32, (G_DEV, DEV), 0) + 1
    hot = jnp.concatenate([one_hot(want == offs[k:k + 1]) for k in range(CAP)], axis=1)
    out_ref[...] = pick(hot, jnp.concatenate([got_ref[pl.ds(k, DEV, stride=SLOTS), :] for k in range(CAP)], axis=0))


SMEM = pl.BlockSpec(memory_space=pltpu.SMEM)
VMEM = pl.BlockSpec(memory_space=pltpu.VMEM)
HBM = pl.BlockSpec(memory_space=pltpu.HBM)
LIMIT = 40 * 1024 * 1024


def f32(*shape):
    return jax.ShapeDtypeStruct(shape, F32)


def call(kernel, name, ins, outs, scratch, flops, moved):
    return pl.pallas_call(
        kernel,
        in_specs=ins,
        out_specs=[VMEM] * len(outs),
        out_shape=outs,
        scratch_shapes=scratch,
        compiler_params=pltpu.CompilerParams(vmem_limit_bytes=LIMIT),
        cost_estimate=pl.CostEstimate(flops=flops, bytes_accessed=moved, transcendentals=0),
        name=name,
    )


def per_device(fields, sources, conductivity, omegas, tx_bricks, owner_map, row_brick, row_offset):
    fields_in, sources_in, conductivity_in, omegas_in = fields, sources, conductivity, omegas
    fields, sources, conductivity, omegas = (
        pltpu.with_memory_space_constraint(x, pltpu.HBM) for x in (fields, sources, conductivity, omegas)
    )
    with_next = [(i, (i + 1) % BRICK) for i in range(1, BRICK, 2)]
    with_last = [(i, i + 1) for i in range(0, BRICK, 2)]
    with_next, with_last = (pairs + [(b, a) for a, b in pairs] for pairs in (with_next, with_last))
    pay = f32(8, NY, NZ)
    packed = f32(DEV * SLOTS, NZ)
    dma = pltpu.SemaphoreType.DMA
    one_e, two_e = call(
        field_halo_kernel, "field_halo", [HBM], [pay, pay],
        [pltpu.VMEM((NF, 2, 2, NY, NZ), F32), pltpu.VMEM((NF, 2, 3, NY, NZ), F32), dma((2 * NF,))], 400_000, 1_200_000,
    )(fields)
    gone_e = lax.ppermute(one_e, BRICK_AXES, with_next)
    gtwo_e = lax.ppermute(two_e, BRICK_AXES, with_last)
    one_r, two_r = call(
        residual_halo_kernel, "residual_halo", [HBM] * 4, [pay, pay],
        [
            pltpu.SMEM((NF,), F32),
            pltpu.VMEM((NF, 2, 3, 2, NY, NZ), F32),
            pltpu.VMEM((NF, 2, 3, 2, NY, NZ), F32),
            pltpu.VMEM((NF, 2, 2, NY, NZ), F32),
            pltpu.VMEM((NF, 2, 3, NY, NZ), F32),
            pltpu.VMEM((2, NY, NZ), F32),
            dma((11,)),
        ], 2_000_000, 3_000_000,
    )(omegas, fields, sources, conductivity)
    gone_r = lax.ppermute(one_r, BRICK_AXES, with_next)
    gtwo_r = lax.ppermute(two_r, BRICK_AXES, with_last)
    fields_v, sources_v, conductivity_v, _ = lax.optimization_barrier((fields_in, sources_in, conductivity_in, two_r))
    fields_v, sources_v, conductivity_v = (
        pltpu.with_memory_space_constraint(x, pltpu.VMEM) for x in (fields_v, sources_v, conductivity_v)
    )
    part, slot, loc, own_r = call(
        main_kernel, "interior", [SMEM, SMEM] + [VMEM] * 6,
        [packed, jax.ShapeDtypeStruct((8, ROWS), I32), f32(ROWS, NZ), pay],
        [
            pltpu.VMEM((12, PL + 1, NY + PAD, NZ), F32),
            pltpu.VMEM((8, PAD + NY, NZ), F32),
            pltpu.VMEM((4, NY, NZ), F32),
        ], 60_000_000, 8_000_000,
    )(
        omegas_in, tx_bricks, fields_v, sources_v, conductivity_v,
        row_brick.reshape(1, ROWS), row_offset, owner_map.reshape(1, DEV),
    )
    part, rest, fac = call(
        field_fix_kernel, "field_fix", [SMEM, SMEM] + [VMEM] * 10,
        [packed, f32(2, NY, NZ), f32(20, NY, NZ)], [pltpu.VMEM((2 * NY, NZ), F32)], 20_000_000, 4_000_000,
    )(omegas_in, tx_bricks, fields_v, conductivity_v, loc, one_e, two_e, own_r, gone_e, gtwo_e, slot, part)
    (send,) = call(
        residual_fix_kernel, "residual_fix", [VMEM] * 6, [packed], [pltpu.VMEM((2 * NY, NZ), F32)], 20_000_000, 3_000_000,
    )(fac, rest, gone_r, gtwo_r, slot, part)
    got = lax.all_to_all(send.reshape(DEV, 1, SLOTS * NZ), SWAP_AXES, 0, 0, tiled=True).reshape(DEV * SLOTS, NZ)
    return pl.pallas_call(
        owner_kernel,
        in_specs=[VMEM],
        out_specs=VMEM,
        out_shape=f32(G_DEV, NZ),
        compiler_params=pltpu.CompilerParams(vmem_limit_bytes=LIMIT),
        name="owner_sum",
    )(got)


def solution(mesh):
    grid = Mesh(mesh.devices.reshape(4, 2, 4, 4), ("y", "core", "x", "z"))
    return jax.shard_map(
        per_device,
        mesh=grid,
        in_specs=(
            P(TX_AXES, None, None, None, BRICK_AXES, None, None),
            P(TX_AXES, None, None, None, BRICK_AXES, None, None),
            P(TX_AXES, BRICK_AXES, None, None),
            P(),
            P(),
            P(),
            P(TX_AXES, BRICK_AXES, None),
            P(TX_AXES, BRICK_AXES),
        ),
        out_specs=P(TX_AXES + BRICK_AXES, None),
        check_vma=False,
    )
```

```python
import jax
import jax.numpy as jnp
from jax import lax
from jax.experimental import pallas as pl
from jax.experimental.pallas import tpu as pltpu
from jax.sharding import Mesh, PartitionSpec as P

PL, NY, NZ, NF = 8, 64, 128, 2
ROWS = PL * NY
G_DEV = 32
CAP = 8
DEV = 128
SLOTS = CAP + 1
BRICK = 16
TX_AXES, BRICK_AXES = ("y", "core"), ("x", "z")
SWAP_AXES = ("core", "x", "z", "y")
PAD = 8
CH = 16
F32, BF16, I32 = jnp.float32, jnp.bfloat16, jnp.int32
SCALE = 0.003


def fy(v):
    rows = lax.broadcasted_iota(I32, v.shape, 0)
    return jnp.where(rows == NY - 1, 0.0, pltpu.roll(v, NY - 1, 0)) - v


def by(v):
    rows = lax.broadcasted_iota(I32, v.shape, 0)
    return v - jnp.where(rows == 0, 0.0, pltpu.roll(v, 1, 0))


def fz(v):
    lanes = lax.broadcasted_iota(I32, v.shape, 1)
    return jnp.where(lanes == NZ - 1, 0.0, pltpu.roll(v, NZ - 1, 1)) - v


def bz(v):
    lanes = lax.broadcasted_iota(I32, v.shape, 1)
    return v - jnp.where(lanes == 0, 0.0, pltpu.roll(v, 1, 1))


def q_of(vx, vy, vz):
    return fz(vx) + vz, vy + fy(vx)


def rotate(curl, part, weight, other):
    return curl - weight * other if part == 0 else curl + weight * other


def signed(part, value):
    return value if part == 1 else -value


def odd_brick():
    return (lax.axis_index(BRICK_AXES) & 1) == 1


def field_halo_kernel(e_hbm, one_ref, two_ref, lo_ref, hi_ref, sems):
    odd = odd_brick()
    lo = [pltpu.make_async_copy(e_hbm.at[0, f, :, pl.ds(1, 2), 0], lo_ref.at[f], sems.at[f]) for f in range(NF)]
    hi = [pltpu.make_async_copy(e_hbm.at[0, f, :, :, PL - 1], hi_ref.at[f], sems.at[NF + f]) for f in range(NF)]
    for f in range(NF):
        hi[f].start()
        lo[f].start()
    for f in range(NF):
        hi[f].wait()
        lo[f].wait()
        for part in range(2):
            q = q_of(*(hi_ref[f, part, c] for c in range(3)))
            for c in range(2):
                at = 2 * (2 * f + part) + c
                one_ref[at] = jnp.where(odd, q[c], lo_ref[f, part, c])
                two_ref[at] = jnp.where(odd, lo_ref[f, part, c], q[c])


def residual_halo_kernel(om_hbm, e_hbm, s_hbm, c_hbm, one_ref, two_ref, om_ref, elo_ref, ehi_ref, slo_ref, shi_ref, cc_ref, sems):
    odd = odd_brick()
    small = [
        pltpu.make_async_copy(om_hbm, om_ref, sems.at[8]),
        pltpu.make_async_copy(c_hbm.at[0, 0], cc_ref.at[0], sems.at[9]),
        pltpu.make_async_copy(c_hbm.at[0, PL - 1], cc_ref.at[1], sems.at[10]),
    ]
    big = [
        [
            pltpu.make_async_copy(e_hbm.at[0, f, :, :, pl.ds(0, 2)], elo_ref.at[f], sems.at[4 * f]),
            pltpu.make_async_copy(s_hbm.at[0, f, :, pl.ds(1, 2), 0], slo_ref.at[f], sems.at[4 * f + 1]),
            pltpu.make_async_copy(e_hbm.at[0, f, :, :, pl.ds(PL - 2, 2)], ehi_ref.at[f], sems.at[4 * f + 2]),
            pltpu.make_async_copy(s_hbm.at[0, f, :, :, PL - 1], shi_ref.at[f], sems.at[4 * f + 3]),
        ]
        for f in range(NF)
    ]
    for copy in small + big[0] + big[1]:
        copy.start()
    for copy in small:
        copy.wait()
    for f in range(NF):
        for copy in big[f]:
            copy.wait()
        om = om_ref[f]
        for part in range(2):
            ch = 2 * f + part
            vx, vy, vz = (elo_ref[f, part, c, 0] for c in range(3))
            hx = fy(vz) - fz(vy)
            hy = fz(vx) - (elo_ref[f, part, 2, 1] - vz)
            hz = (elo_ref[f, part, 1, 1] - vy) - fy(vx)
            w = om * cc_ref[0]
            dy = rotate(bz(hx) - hz, part, w, elo_ref[f, 1 - part, 1, 0]) - slo_ref[f, part, 0]
            dz = rotate(hy - by(hx), part, w, elo_ref[f, 1 - part, 2, 0]) - slo_ref[f, part, 1]
            ux, uy, uz = (ehi_ref[f, part, c, 0] for c in range(3))
            vx, vy, vz = (ehi_ref[f, part, c, 1] for c in range(3))
            hy, qz = q_of(vx, vy, vz)
            hz = -qz
            hx = fy(vz) - fz(vy)
            gy = fz(ux) - (vz - uz)
            gz = (vy - uy) - fy(ux)
            w = om * cc_ref[1]
            o = [ehi_ref[f, 1 - part, c, 1] for c in range(3)]
            rx = rotate(by(hz) - bz(hy), part, w, o[0]) - shi_ref[f, part, 0]
            ry = rotate(bz(hx) - (hz - gz), part, w, o[1]) - shi_ref[f, part, 1]
            rz = rotate((hy - gy) - by(hx), part, w, o[2]) - shi_ref[f, part, 2]
            sy, sz = q_of(rx, ry, rz)
            one_ref[2 * ch] = jnp.where(odd, sy, dy)
            one_ref[2 * ch + 1] = jnp.where(odd, sz, dz)
            two_ref[2 * ch] = jnp.where(odd, dy, sy)
            two_ref[2 * ch + 1] = jnp.where(odd, dz, sz)


def one_hot(cond):
    return jnp.where(cond, 1.0, 0.0).astype(BF16)


def dot(a, b):
    return jnp.dot(a, b, preferred_element_type=F32)


def pick(hot, v):
    hi = v.astype(BF16)
    low = (v - hi.astype(F32)).astype(BF16)
    both = dot(hot, jnp.concatenate([hi, low], axis=1))
    return both[:, 0:NZ] + both[:, NZ:2 * NZ]


def place(tb_ref):
    brick = lax.axis_index(BRICK_AXES)
    span = tb_ref[lax.axis_index(TX_AXES)]
    live = jnp.where(brick < span, 1.0, 0.0).astype(F32)
    low = jnp.where(brick > 0, 1.0, 0.0).astype(F32)
    nxt = jnp.where(brick + 1 < span, 1.0, 0.0).astype(F32)
    return live, low, nxt


def curl(get, h_ref, g_ref, p, y, ch):
    lanes = lax.broadcasted_iota(I32, (CH, NZ), 1)

    def nz_(v):
        return jnp.where(lanes == NZ - 1, 0.0, pltpu.roll(v, NZ - 1, 1))

    def pz_(v):
        return jnp.where(lanes == 0, 0.0, pltpu.roll(v, 1, 1))

    vx, vy, vz = (get(c, p, y) for c in range(3))
    hx = (get(2, p, y + 1) - vz) - (nz_(vy) - vy)
    hy = (nz_(vx) - vx) - (get(2, p + 1, y) - vz)
    hz = (get(1, p + 1, y) - vy) - (get(0, p, y + 1) - vx)
    gy = g_ref[ch, y:y + CH]
    gz = h_ref[2 * ch + 1, PAD + y:PAD + y + CH]
    h_ref[2 * ch, PAD + y:PAD + y + CH] = hx
    h_ref[2 * ch + 1, PAD + y:PAD + y + CH] = hz
    g_ref[ch, y:y + CH] = hy
    hxp = h_ref[2 * ch, PAD + y - 1:PAD + y - 1 + CH]
    hzp = h_ref[2 * ch + 1, PAD + y - 1:PAD + y - 1 + CH]
    cx = (hz - hzp) - (hy - pz_(hy))
    cy = (hx - pz_(hx)) - (hz - gz)
    cz = (hy - gy) - (hx - hxp)
    return (vx, vy, vz), (cx, cy, cz)


def residual_kernel(om_ref, e_ref, s_ref, c_ref, rb_ref, ro_ref, own_ref, r_ref, slot_ref, index_ref, h_ref, g_ref):
    zero = jnp.zeros((NY, NZ), F32)
    zpad = jnp.zeros((PAD, NZ), F32)
    for i in range(12):
        for p in range(PL):
            r_ref[i, p, NY:NY + PAD] = zpad
    for i in range(8):
        h_ref[i, 0:PAD] = zpad
        h_ref[i, PAD:PAD + NY] = zero
    for i in range(4):
        g_ref[i] = zero

    bt = lax.broadcasted_iota(I32, (DEV, ROWS), 0) == rb_ref[...]
    hot = one_hot(bt)
    before = one_hot(lax.broadcasted_iota(I32, (ROWS, ROWS), 0) < lax.broadcasted_iota(I32, (ROWS, ROWS), 1))
    counts = dot(hot, before)
    rank = jnp.sum(jnp.where(bt, counts, 0.0), axis=0, keepdims=True)
    own8 = jnp.broadcast_to(own_ref[...].astype(F32), (8, DEV)).astype(BF16)
    dest = dot(own8, hot)[0:1].astype(I32)
    dest = ((dest >> 4) & 1) * 64 + ((dest >> 2) & 3) * 16 + (dest & 3) * 4 + (dest >> 5)
    rank = rank.astype(I32)
    slot = dest * SLOTS + rank
    slot_ref[...] = jnp.broadcast_to(slot, (8, ROWS))
    codes = jnp.where(lax.broadcasted_iota(I32, (NZ, ROWS), 0) == rank, (ro_ref[...] + 1).astype(F32), 0.0).astype(BF16)
    mine = one_hot(lax.broadcasted_iota(I32, (DEV, ROWS), 0) == dest)
    index_ref[...] = lax.dot_general(mine, codes, (((1,), (1,)), ((), ())), preferred_element_type=F32)

    rows = lax.broadcasted_iota(I32, (CH, NZ), 0)

    def step(p, carry):
        after = jnp.minimum(p + 1, PL - 1)
        inside = jnp.where(p < PL - 1, 1.0, 0.0).astype(F32)
        for y in range(0, NY, CH):
            sig = c_ref[0, p, y:y + CH]
            for f in range(NF):
                w = om_ref[f] * sig
                for part in range(2):
                    ch = 2 * f + part

                    def get(c, q, r):
                        if q is not p:
                            return e_ref[0, f, part, c, after, r:r + CH] * inside
                        if r + CH <= NY:
                            return e_ref[0, f, part, c, p, r:r + CH]
                        last = e_ref[0, f, part, c, p, NY - CH:NY]
                        return jnp.where(rows == CH - 1, 0.0, pltpu.roll(last, CH - 1, 0))

                    _, cs = curl(get, h_ref, g_ref, p, y, ch)
                    for c in range(3):
                        o = e_ref[0, f, 1 - part, c, p, y:y + CH]
                        r_ref[3 * ch + c, p, y:y + CH] = rotate(cs[c], part, w, o) - s_ref[0, f, part, c, p, y:y + CH]
        return carry

    lax.fori_loop(0, PL, step, 0)
    for ch in range(4):
        r_ref[3 * ch + 1, PL, 0:NY] = h_ref[2 * ch + 1, PAD:PAD + NY]
        r_ref[3 * ch + 2, PL, 0:NY] = -g_ref[ch]


def adjoint_kernel(
    om_ref, tb_ref, e_ref, c_ref, slot_ref, index_ref, gone_ref, gtwo_ref, rin_ref,
    part_ref, rest_ref, fac_ref, r_ref, h_ref, g_ref, loc_ref,
):
    live, low, nxt = place(tb_ref)
    odd = odd_brick()
    end = PL - 1
    zpad = jnp.zeros((PAD, NZ), F32)
    for i in range(8):
        h_ref[i, 0:PAD] = zpad
    for f in range(NF):
        weight = SCALE * om_ref[f] * live
        for part in range(2):
            ch = 2 * f + part
            x, y, z = 3 * ch, 3 * ch + 1, 3 * ch + 2
            ey, ez = e_ref[0, f, part, 1, 0], e_ref[0, f, part, 2, 0]
            first = [gone_ref[2 * ch + c] for c in range(2)]
            second = [gtwo_ref[2 * ch + c] for c in range(2)]
            qy, qz = (jnp.where(odd, second[c], first[c]) for c in range(2))
            ry = rin_ref[y, 0, 0:NY] + low * (ey - qz)
            rz = rin_ref[z, 0, 0:NY] + low * (ez - qy)
            r_ref[y, 0, 0:NY] = ry
            r_ref[z, 0, 0:NY] = rz
            div = by(ey) + bz(ez)
            g_ref[ch] = low * (fz(div) - ez - rz)
            h_ref[2 * ch + 1, PAD:PAD + NY] = low * (ry - fy(div) + ey)
            ey, ez = (nxt * jnp.where(odd, first[c], second[c]) for c in range(2))
            r_ref[x, end, 0:NY] = rin_ref[x, end, 0:NY] + (by(ey) + bz(ez))
            r_ref[y, end, 0:NY] = rin_ref[y, end, 0:NY] - ey
            r_ref[z, end, 0:NY] = rin_ref[z, end, 0:NY] - ez
            r_ref[y, PL, 0:NY] = nxt * rin_ref[y, PL, 0:NY] + ey
            r_ref[z, PL, 0:NY] = nxt * rin_ref[z, PL, 0:NY] + ez
            scale = -signed(part, weight) * low
            fac_ref[2 * ch] = scale * e_ref[0, f, 1 - part, 2, 0]
            fac_ref[2 * ch + 1] = scale * e_ref[0, f, 1 - part, 1, 0]
            scale = signed(part, weight) * nxt
            for c in range(3):
                fac_ref[8 + 3 * ch + c] = scale * e_ref[0, f, 1 - part, c, end]

    def step(p, carry):
        for y in range(0, NY, CH):
            sig = c_ref[0, p, y:y + CH]
            acc = jnp.zeros((CH, NZ), F32)
            for f in range(NF):
                om = om_ref[f]
                tot = jnp.zeros((CH, NZ), F32)
                dia = jnp.zeros((CH, NZ), F32)
                for part in range(2):
                    ch = 2 * f + part
                    vs, cs = curl(lambda c, q, r: r_ref[3 * ch + c, q, r:r + CH], h_ref, g_ref, p, y, ch)
                    o = [e_ref[0, f, 1 - part, c, p, y:y + CH] for c in range(3)]
                    s = [e_ref[0, f, part, c, p, y:y + CH] for c in range(3)]
                    tot = tot + signed(part, o[0] * cs[0] + o[1] * cs[1] + o[2] * cs[2])
                    dia = dia + (s[0] * vs[0] + s[1] * vs[1] + s[2] * vs[2])
                acc = acc + (SCALE * om * live) * (tot + (om * sig) * dia)
            loc_ref[pl.ds(pl.multiple_of(p * NY + y, CH), CH), :] = acc
        return carry

    lax.fori_loop(0, PL, step, 0)

    rest_ref[0] = loc_ref[0:NY]
    rest_ref[1] = loc_ref[ROWS - NY:ROWS]
    lo, hi = NY, ROWS - NY
    at = lax.broadcasted_iota(I32, (DEV * SLOTS, hi - lo), 0)
    part_ref[...] = pick(one_hot(at == slot_ref[0:1, lo:hi]), loc_ref[lo:hi])
    part_ref[pl.ds(CAP, DEV, stride=SLOTS), :] = index_ref[...]


def residual_fix_kernel(fac_ref, rest_ref, gone_ref, gtwo_ref, slot_ref, part_ref, out_ref, two_ref):
    odd = odd_brick()
    low, high = rest_ref[0], rest_ref[1]
    for ch in range(4):
        first = [gone_ref[2 * ch + c] for c in range(2)]
        second = [gtwo_ref[2 * ch + c] for c in range(2)]
        qy, qz = (jnp.where(odd, second[c], first[c]) for c in range(2))
        ry, rz = (jnp.where(odd, first[c], second[c]) for c in range(2))
        low = low + (fac_ref[2 * ch] * qy + fac_ref[2 * ch + 1] * qz)
        o = [fac_ref[8 + 3 * ch + c] for c in range(3)]
        high = high + (o[0] * (by(ry) + bz(rz)) - o[1] * ry - o[2] * rz)
    two_ref[0:NY] = low
    two_ref[NY:2 * NY] = high
    at = lax.broadcasted_iota(I32, (DEV * SLOTS, NY), 0)
    hot = jnp.concatenate([one_hot(at == slot_ref[0:1, 0:NY]), one_hot(at == slot_ref[0:1, ROWS - NY:ROWS])], axis=1)
    out_ref[...] = part_ref[...] + pick(hot, two_ref[...])


def owner_kernel(got_ref, out_ref):
    codes = got_ref[pl.ds(CAP, DEV, stride=SLOTS), :]
    offs = codes.T[0:CAP].astype(I32)
    want = lax.broadcasted_iota(I32, (G_DEV, DEV), 0) + 1
    hot = jnp.concatenate([one_hot(want == offs[k:k + 1]) for k in range(CAP)], axis=1)
    out_ref[...] = pick(hot, jnp.concatenate([got_ref[pl.ds(k, DEV, stride=SLOTS), :] for k in range(CAP)], axis=0))


SMEM = pl.BlockSpec(memory_space=pltpu.SMEM)
VMEM = pl.BlockSpec(memory_space=pltpu.VMEM)
HBM = pl.BlockSpec(memory_space=pltpu.HBM)
LIMIT = 40 * 1024 * 1024


def f32(*shape):
    return jax.ShapeDtypeStruct(shape, F32)


def call(kernel, name, ins, outs, scratch, flops, moved):
    return pl.pallas_call(
        kernel,
        in_specs=ins,
        out_specs=[VMEM] * len(outs),
        out_shape=outs,
        scratch_shapes=scratch,
        compiler_params=pltpu.CompilerParams(vmem_limit_bytes=LIMIT),
        cost_estimate=pl.CostEstimate(flops=flops, bytes_accessed=moved, transcendentals=0),
        name=name,
    )


def per_device(fields, sources, conductivity, omegas, tx_bricks, owner_map, row_brick, row_offset):
    fields_in, sources_in, conductivity_in, omegas_in = fields, sources, conductivity, omegas
    fields, sources, conductivity, omegas = (
        pltpu.with_memory_space_constraint(x, pltpu.HBM) for x in (fields, sources, conductivity, omegas)
    )
    with_next = [(i, (i + 1) % BRICK) for i in range(1, BRICK, 2)]
    with_last = [(i, i + 1) for i in range(0, BRICK, 2)]
    with_next, with_last = (pairs + [(b, a) for a, b in pairs] for pairs in (with_next, with_last))
    pay = f32(8, NY, NZ)
    packed = f32(DEV * SLOTS, NZ)
    dma = pltpu.SemaphoreType.DMA
    one_e, two_e = call(
        field_halo_kernel, "field_halo", [HBM], [pay, pay],
        [pltpu.VMEM((NF, 2, 2, NY, NZ), F32), pltpu.VMEM((NF, 2, 3, NY, NZ), F32), dma((2 * NF,))], 400_000, 1_200_000,
    )(fields)
    gone_e = lax.ppermute(one_e, BRICK_AXES, with_next)
    gtwo_e = lax.ppermute(two_e, BRICK_AXES, with_last)
    one_r, two_r = call(
        residual_halo_kernel, "residual_halo", [HBM] * 4, [pay, pay],
        [
            pltpu.SMEM((NF,), F32),
            pltpu.VMEM((NF, 2, 3, 2, NY, NZ), F32),
            pltpu.VMEM((NF, 2, 3, 2, NY, NZ), F32),
            pltpu.VMEM((NF, 2, 2, NY, NZ), F32),
            pltpu.VMEM((NF, 2, 3, NY, NZ), F32),
            pltpu.VMEM((2, NY, NZ), F32),
            dma((11,)),
        ], 2_000_000, 3_000_000,
    )(omegas, fields, sources, conductivity)
    gone_r = lax.ppermute(one_r, BRICK_AXES, with_next)
    gtwo_r = lax.ppermute(two_r, BRICK_AXES, with_last)
    fields_v, sources_v, conductivity_v, _ = lax.optimization_barrier((fields_in, sources_in, conductivity_in, two_r))
    fields_v, sources_v, conductivity_v = (
        pltpu.with_memory_space_constraint(x, pltpu.VMEM) for x in (fields_v, sources_v, conductivity_v)
    )
    halo = [pltpu.VMEM((8, PAD + NY, NZ), F32), pltpu.VMEM((4, NY, NZ), F32)]
    r, slot, index = call(
        residual_kernel, "residual", [SMEM] + [VMEM] * 6,
        [f32(12, PL + 1, NY + PAD, NZ), jax.ShapeDtypeStruct((8, ROWS), I32), f32(DEV, NZ)],
        halo, 30_000_000, 8_000_000,
    )(
        omegas_in, fields_v, sources_v, conductivity_v,
        row_brick.reshape(1, ROWS), row_offset, owner_map.reshape(1, DEV),
    )
    part, rest, fac, _ = pl.pallas_call(
        adjoint_kernel,
        in_specs=[SMEM, SMEM] + [VMEM] * 7,
        out_specs=[VMEM] * 4,
        out_shape=[packed, f32(2, NY, NZ), f32(20, NY, NZ), f32(12, PL + 1, NY + PAD, NZ)],
        input_output_aliases={8: 3},
        scratch_shapes=halo + [pltpu.VMEM((ROWS, NZ), F32)],
        compiler_params=pltpu.CompilerParams(vmem_limit_bytes=LIMIT),
        cost_estimate=pl.CostEstimate(flops=40_000_000, bytes_accessed=8_000_000, transcendentals=0),
        name="adjoint",
    )(omegas_in, tx_bricks, fields_v, conductivity_v, slot, index, gone_e, gtwo_e, r)
    (send,) = call(
        residual_fix_kernel, "residual_fix", [VMEM] * 6, [packed], [pltpu.VMEM((2 * NY, NZ), F32)], 20_000_000, 3_000_000,
    )(fac, rest, gone_r, gtwo_r, slot, part)
    got = lax.all_to_all(send.reshape(DEV, 1, SLOTS * NZ), SWAP_AXES, 0, 0, tiled=True).reshape(DEV * SLOTS, NZ)
    return pl.pallas_call(
        owner_kernel,
        in_specs=[VMEM],
        out_specs=VMEM,
        out_shape=f32(G_DEV, NZ),
        compiler_params=pltpu.CompilerParams(vmem_limit_bytes=LIMIT),
        name="owner_sum",
    )(got)


def solution(mesh):
    grid = Mesh(mesh.devices.reshape(4, 2, 4, 4), ("y", "core", "x", "z"))
    return jax.shard_map(
        per_device,
        mesh=grid,
        in_specs=(
            P(TX_AXES, None, None, None, BRICK_AXES, None, None),
            P(TX_AXES, None, None, None, BRICK_AXES, None, None),
            P(TX_AXES, BRICK_AXES, None, None),
            P(),
            P(),
            P(),
            P(TX_AXES, BRICK_AXES, None),
            P(TX_AXES, BRICK_AXES),
        ),
        out_specs=P(TX_AXES + BRICK_AXES, None),
        check_vma=False,
    )
```

```python
import jax
import jax.numpy as jnp
from jax import lax
from jax.experimental import pallas as pl
from jax.experimental.pallas import tpu as pltpu
from jax.sharding import Mesh, PartitionSpec as P

PL, NY, NZ, NF = 8, 64, 128, 2
ROWS = PL * NY
G_DEV = 32
CAP = 8
DEV = 128
SLOTS = CAP + 1
BRICK = 16
TX_AXES, BRICK_AXES = ("y", "core"), ("x", "z")
SWAP_AXES = ("core", "y", "x", "z")
PAD = 8
CH = 16
F32, BF16, I32 = jnp.float32, jnp.bfloat16, jnp.int32
SCALE = 0.003


def fy(v):
    rows = lax.broadcasted_iota(I32, v.shape, 0)
    return jnp.where(rows == NY - 1, 0.0, pltpu.roll(v, NY - 1, 0)) - v


def by(v):
    rows = lax.broadcasted_iota(I32, v.shape, 0)
    return v - jnp.where(rows == 0, 0.0, pltpu.roll(v, 1, 0))


def fz(v):
    lanes = lax.broadcasted_iota(I32, v.shape, 1)
    return jnp.where(lanes == NZ - 1, 0.0, pltpu.roll(v, NZ - 1, 1)) - v


def bz(v):
    lanes = lax.broadcasted_iota(I32, v.shape, 1)
    return v - jnp.where(lanes == 0, 0.0, pltpu.roll(v, 1, 1))


def q_of(vx, vy, vz):
    return fz(vx) + vz, vy + fy(vx)


def rotate(curl, part, weight, other):
    return curl - weight * other if part == 0 else curl + weight * other


def signed(part, value):
    return value if part == 1 else -value


def odd_brick():
    return (lax.axis_index(BRICK_AXES) & 1) == 1


def field_halo_kernel(e_hbm, one_ref, two_ref, lo_ref, hi_ref, sems):
    odd = odd_brick()
    lo = [pltpu.make_async_copy(e_hbm.at[0, f, :, pl.ds(1, 2), 0], lo_ref.at[f], sems.at[f]) for f in range(NF)]
    hi = [pltpu.make_async_copy(e_hbm.at[0, f, :, :, PL - 1], hi_ref.at[f], sems.at[NF + f]) for f in range(NF)]
    for f in range(NF):
        hi[f].start()
        lo[f].start()
    for f in range(NF):
        hi[f].wait()
        lo[f].wait()
        for part in range(2):
            q = q_of(*(hi_ref[f, part, c] for c in range(3)))
            for c in range(2):
                at = 2 * (2 * f + part) + c
                one_ref[at] = jnp.where(odd, q[c], lo_ref[f, part, c])
                two_ref[at] = jnp.where(odd, lo_ref[f, part, c], q[c])


def residual_halo_kernel(om_hbm, e_hbm, s_hbm, c_hbm, one_ref, two_ref, om_ref, elo_ref, ehi_ref, slo_ref, shi_ref, cc_ref, sems):
    odd = odd_brick()
    small = [
        pltpu.make_async_copy(om_hbm, om_ref, sems.at[8]),
        pltpu.make_async_copy(c_hbm.at[0, 0], cc_ref.at[0], sems.at[9]),
        pltpu.make_async_copy(c_hbm.at[0, PL - 1], cc_ref.at[1], sems.at[10]),
    ]
    big = [
        [
            pltpu.make_async_copy(e_hbm.at[0, f, :, :, pl.ds(0, 2)], elo_ref.at[f], sems.at[4 * f]),
            pltpu.make_async_copy(s_hbm.at[0, f, :, pl.ds(1, 2), 0], slo_ref.at[f], sems.at[4 * f + 1]),
            pltpu.make_async_copy(e_hbm.at[0, f, :, :, pl.ds(PL - 2, 2)], ehi_ref.at[f], sems.at[4 * f + 2]),
            pltpu.make_async_copy(s_hbm.at[0, f, :, :, PL - 1], shi_ref.at[f], sems.at[4 * f + 3]),
        ]
        for f in range(NF)
    ]
    for copy in small + big[0] + big[1]:
        copy.start()
    for copy in small:
        copy.wait()
    for f in range(NF):
        for copy in big[f]:
            copy.wait()
        om = om_ref[f]
        for part in range(2):
            ch = 2 * f + part
            vx, vy, vz = (elo_ref[f, part, c, 0] for c in range(3))
            hx = fy(vz) - fz(vy)
            hy = fz(vx) - (elo_ref[f, part, 2, 1] - vz)
            hz = (elo_ref[f, part, 1, 1] - vy) - fy(vx)
            w = om * cc_ref[0]
            dy = rotate(bz(hx) - hz, part, w, elo_ref[f, 1 - part, 1, 0]) - slo_ref[f, part, 0]
            dz = rotate(hy - by(hx), part, w, elo_ref[f, 1 - part, 2, 0]) - slo_ref[f, part, 1]
            ux, uy, uz = (ehi_ref[f, part, c, 0] for c in range(3))
            vx, vy, vz = (ehi_ref[f, part, c, 1] for c in range(3))
            hy, qz = q_of(vx, vy, vz)
            hz = -qz
            hx = fy(vz) - fz(vy)
            gy = fz(ux) - (vz - uz)
            gz = (vy - uy) - fy(ux)
            w = om * cc_ref[1]
            o = [ehi_ref[f, 1 - part, c, 1] for c in range(3)]
            rx = rotate(by(hz) - bz(hy), part, w, o[0]) - shi_ref[f, part, 0]
            ry = rotate(bz(hx) - (hz - gz), part, w, o[1]) - shi_ref[f, part, 1]
            rz = rotate((hy - gy) - by(hx), part, w, o[2]) - shi_ref[f, part, 2]
            sy, sz = q_of(rx, ry, rz)
            one_ref[2 * ch] = jnp.where(odd, sy, dy)
            one_ref[2 * ch + 1] = jnp.where(odd, sz, dz)
            two_ref[2 * ch] = jnp.where(odd, dy, sy)
            two_ref[2 * ch + 1] = jnp.where(odd, dz, sz)


def one_hot(cond):
    return jnp.where(cond, 1.0, 0.0).astype(BF16)


def dot(a, b):
    return jnp.dot(a, b, preferred_element_type=F32)


def pick(hot, v):
    hi = v.astype(BF16)
    low = (v - hi.astype(F32)).astype(BF16)
    both = dot(hot, jnp.concatenate([hi, low], axis=1))
    return both[:, 0:NZ] + both[:, NZ:2 * NZ]


def place(tb_ref):
    brick = lax.axis_index(BRICK_AXES)
    span = tb_ref[lax.axis_index(TX_AXES)]
    live = jnp.where(brick < span, 1.0, 0.0).astype(F32)
    low = jnp.where(brick > 0, 1.0, 0.0).astype(F32)
    nxt = jnp.where(brick + 1 < span, 1.0, 0.0).astype(F32)
    return live, low, nxt


def curl(get, h_ref, g_ref, p, y, ch):
    lanes = lax.broadcasted_iota(I32, (CH, NZ), 1)

    def nz_(v):
        return jnp.where(lanes == NZ - 1, 0.0, pltpu.roll(v, NZ - 1, 1))

    def pz_(v):
        return jnp.where(lanes == 0, 0.0, pltpu.roll(v, 1, 1))

    vx, vy, vz = (get(c, p, y) for c in range(3))
    hx = (get(2, p, y + 1) - vz) - (nz_(vy) - vy)
    hy = (nz_(vx) - vx) - (get(2, p + 1, y) - vz)
    hz = (get(1, p + 1, y) - vy) - (get(0, p, y + 1) - vx)
    gy = g_ref[ch, y:y + CH]
    gz = h_ref[2 * ch + 1, PAD + y:PAD + y + CH]
    h_ref[2 * ch, PAD + y:PAD + y + CH] = hx
    h_ref[2 * ch + 1, PAD + y:PAD + y + CH] = hz
    g_ref[ch, y:y + CH] = hy
    hxp = h_ref[2 * ch, PAD + y - 1:PAD + y - 1 + CH]
    hzp = h_ref[2 * ch + 1, PAD + y - 1:PAD + y - 1 + CH]
    cx = (hz - hzp) - (hy - pz_(hy))
    cy = (hx - pz_(hx)) - (hz - gz)
    cz = (hy - gy) - (hx - hxp)
    return (vx, vy, vz), (cx, cy, cz)


def residual_kernel(om_ref, e_ref, s_ref, c_ref, rb_ref, ro_ref, own_ref, r_ref, slot_ref, index_ref, h_ref, g_ref):
    zero = jnp.zeros((NY, NZ), F32)
    zpad = jnp.zeros((PAD, NZ), F32)
    for i in range(12):
        for p in range(PL):
            r_ref[i, p, NY:NY + PAD] = zpad
    for i in range(8):
        h_ref[i, 0:PAD] = zpad
        h_ref[i, PAD:PAD + NY] = zero
    for i in range(4):
        g_ref[i] = zero

    bt = lax.broadcasted_iota(I32, (DEV, ROWS), 0) == rb_ref[...]
    hot = one_hot(bt)
    before = one_hot(lax.broadcasted_iota(I32, (ROWS, ROWS), 0) < lax.broadcasted_iota(I32, (ROWS, ROWS), 1))
    counts = dot(hot, before)
    rank = jnp.sum(jnp.where(bt, counts, 0.0), axis=0, keepdims=True)
    own8 = jnp.broadcast_to(own_ref[...].astype(F32), (8, DEV)).astype(BF16)
    dest = dot(own8, hot)[0:1].astype(I32)
    dest = (dest & 3) * 1 + ((dest >> 2) & 3) * 4 + (dest >> 5) * 16 + ((dest >> 4) & 1) * 64
    rank = rank.astype(I32)
    slot = dest * SLOTS + rank
    slot_ref[...] = jnp.broadcast_to(slot, (8, ROWS))
    codes = jnp.where(lax.broadcasted_iota(I32, (NZ, ROWS), 0) == rank, (ro_ref[...] + 1).astype(F32), 0.0).astype(BF16)
    mine = one_hot(lax.broadcasted_iota(I32, (DEV, ROWS), 0) == dest)
    index_ref[...] = lax.dot_general(mine, codes, (((1,), (1,)), ((), ())), preferred_element_type=F32)

    rows = lax.broadcasted_iota(I32, (CH, NZ), 0)

    def step(p, carry):
        after = jnp.minimum(p + 1, PL - 1)
        inside = jnp.where(p < PL - 1, 1.0, 0.0).astype(F32)
        for y in range(0, NY, CH):
            sig = c_ref[0, p, y:y + CH]
            for f in range(NF):
                w = om_ref[f] * sig
                for part in range(2):
                    ch = 2 * f + part

                    def get(c, q, r):
                        if q is not p:
                            return e_ref[0, f, part, c, after, r:r + CH] * inside
                        if r + CH <= NY:
                            return e_ref[0, f, part, c, p, r:r + CH]
                        last = e_ref[0, f, part, c, p, NY - CH:NY]
                        return jnp.where(rows == CH - 1, 0.0, pltpu.roll(last, CH - 1, 0))

                    _, cs = curl(get, h_ref, g_ref, p, y, ch)
                    for c in range(3):
                        o = e_ref[0, f, 1 - part, c, p, y:y + CH]
                        r_ref[3 * ch + c, p, y:y + CH] = rotate(cs[c], part, w, o) - s_ref[0, f, part, c, p, y:y + CH]
        return carry

    lax.fori_loop(0, PL, step, 0)
    for ch in range(4):
        r_ref[3 * ch + 1, PL, 0:NY] = h_ref[2 * ch + 1, PAD:PAD + NY]
        r_ref[3 * ch + 2, PL, 0:NY] = -g_ref[ch]


def adjoint_kernel(
    om_ref, tb_ref, e_ref, c_ref, slot_ref, index_ref, gone_ref, gtwo_ref, rin_ref,
    part_ref, rest_ref, fac_ref, r_ref, h_ref, g_ref, loc_ref,
):
    live, low, nxt = place(tb_ref)
    odd = odd_brick()
    end = PL - 1
    zpad = jnp.zeros((PAD, NZ), F32)
    for i in range(8):
        h_ref[i, 0:PAD] = zpad
    for f in range(NF):
        weight = SCALE * om_ref[f] * live
        for part in range(2):
            ch = 2 * f + part
            x, y, z = 3 * ch, 3 * ch + 1, 3 * ch + 2
            ey, ez = e_ref[0, f, part, 1, 0], e_ref[0, f, part, 2, 0]
            first = [gone_ref[2 * ch + c] for c in range(2)]
            second = [gtwo_ref[2 * ch + c] for c in range(2)]
            qy, qz = (jnp.where(odd, second[c], first[c]) for c in range(2))
            ry = rin_ref[y, 0, 0:NY] + low * (ey - qz)
            rz = rin_ref[z, 0, 0:NY] + low * (ez - qy)
            r_ref[y, 0, 0:NY] = ry
            r_ref[z, 0, 0:NY] = rz
            div = by(ey) + bz(ez)
            g_ref[ch] = low * (fz(div) - ez - rz)
            h_ref[2 * ch + 1, PAD:PAD + NY] = low * (ry - fy(div) + ey)
            ey, ez = (nxt * jnp.where(odd, first[c], second[c]) for c in range(2))
            r_ref[x, end, 0:NY] = rin_ref[x, end, 0:NY] + (by(ey) + bz(ez))
            r_ref[y, end, 0:NY] = rin_ref[y, end, 0:NY] - ey
            r_ref[z, end, 0:NY] = rin_ref[z, end, 0:NY] - ez
            r_ref[y, PL, 0:NY] = nxt * rin_ref[y, PL, 0:NY] + ey
            r_ref[z, PL, 0:NY] = nxt * rin_ref[z, PL, 0:NY] + ez
            scale = -signed(part, weight) * low
            fac_ref[2 * ch] = scale * e_ref[0, f, 1 - part, 2, 0]
            fac_ref[2 * ch + 1] = scale * e_ref[0, f, 1 - part, 1, 0]
            scale = signed(part, weight) * nxt
            for c in range(3):
                fac_ref[8 + 3 * ch + c] = scale * e_ref[0, f, 1 - part, c, end]

    def step(p, carry):
        for y in range(0, NY, CH):
            sig = c_ref[0, p, y:y + CH]
            acc = jnp.zeros((CH, NZ), F32)
            for f in range(NF):
                om = om_ref[f]
                tot = jnp.zeros((CH, NZ), F32)
                dia = jnp.zeros((CH, NZ), F32)
                for part in range(2):
                    ch = 2 * f + part
                    vs, cs = curl(lambda c, q, r: r_ref[3 * ch + c, q, r:r + CH], h_ref, g_ref, p, y, ch)
                    o = [e_ref[0, f, 1 - part, c, p, y:y + CH] for c in range(3)]
                    s = [e_ref[0, f, part, c, p, y:y + CH] for c in range(3)]
                    tot = tot + signed(part, o[0] * cs[0] + o[1] * cs[1] + o[2] * cs[2])
                    dia = dia + (s[0] * vs[0] + s[1] * vs[1] + s[2] * vs[2])
                acc = acc + (SCALE * om * live) * (tot + (om * sig) * dia)
            loc_ref[pl.ds(pl.multiple_of(p * NY + y, CH), CH), :] = acc
        return carry

    lax.fori_loop(0, PL, step, 0)

    rest_ref[0] = loc_ref[0:NY]
    rest_ref[1] = loc_ref[ROWS - NY:ROWS]
    lo, hi = NY, ROWS - NY
    at = lax.broadcasted_iota(I32, (DEV * SLOTS, hi - lo), 0)
    part_ref[...] = pick(one_hot(at == slot_ref[0:1, lo:hi]), loc_ref[lo:hi])
    part_ref[pl.ds(CAP, DEV, stride=SLOTS), :] = index_ref[...]


def residual_fix_kernel(fac_ref, rest_ref, gone_ref, gtwo_ref, slot_ref, part_ref, out_ref, two_ref):
    odd = odd_brick()
    low, high = rest_ref[0], rest_ref[1]
    for ch in range(4):
        first = [gone_ref[2 * ch + c] for c in range(2)]
        second = [gtwo_ref[2 * ch + c] for c in range(2)]
        qy, qz = (jnp.where(odd, second[c], first[c]) for c in range(2))
        ry, rz = (jnp.where(odd, first[c], second[c]) for c in range(2))
        low = low + (fac_ref[2 * ch] * qy + fac_ref[2 * ch + 1] * qz)
        o = [fac_ref[8 + 3 * ch + c] for c in range(3)]
        high = high + (o[0] * (by(ry) + bz(rz)) - o[1] * ry - o[2] * rz)
    two_ref[0:NY] = low
    two_ref[NY:2 * NY] = high
    at = lax.broadcasted_iota(I32, (DEV * SLOTS, NY), 0)
    hot = jnp.concatenate([one_hot(at == slot_ref[0:1, 0:NY]), one_hot(at == slot_ref[0:1, ROWS - NY:ROWS])], axis=1)
    out_ref[...] = part_ref[...] + pick(hot, two_ref[...])


def owner_kernel(got_ref, out_ref):
    codes = got_ref[pl.ds(CAP, DEV, stride=SLOTS), :]
    offs = codes.T[0:CAP].astype(I32)
    want = lax.broadcasted_iota(I32, (G_DEV, DEV), 0) + 1
    hot = jnp.concatenate([one_hot(want == offs[k:k + 1]) for k in range(CAP)], axis=1)
    out_ref[...] = pick(hot, jnp.concatenate([got_ref[pl.ds(k, DEV, stride=SLOTS), :] for k in range(CAP)], axis=0))


SMEM = pl.BlockSpec(memory_space=pltpu.SMEM)
VMEM = pl.BlockSpec(memory_space=pltpu.VMEM)
HBM = pl.BlockSpec(memory_space=pltpu.HBM)
LIMIT = 40 * 1024 * 1024


def f32(*shape):
    return jax.ShapeDtypeStruct(shape, F32)


def call(kernel, name, ins, outs, scratch, flops, moved):
    return pl.pallas_call(
        kernel,
        in_specs=ins,
        out_specs=[VMEM] * len(outs),
        out_shape=outs,
        scratch_shapes=scratch,
        compiler_params=pltpu.CompilerParams(vmem_limit_bytes=LIMIT),
        cost_estimate=pl.CostEstimate(flops=flops, bytes_accessed=moved, transcendentals=0),
        name=name,
    )


def per_device(fields, sources, conductivity, omegas, tx_bricks, owner_map, row_brick, row_offset):
    fields_in, sources_in, conductivity_in, omegas_in = fields, sources, conductivity, omegas
    fields, sources, conductivity, omegas = (
        pltpu.with_memory_space_constraint(x, pltpu.HBM) for x in (fields, sources, conductivity, omegas)
    )
    with_next = [(i, (i + 1) % BRICK) for i in range(1, BRICK, 2)]
    with_last = [(i, i + 1) for i in range(0, BRICK, 2)]
    with_next, with_last = (pairs + [(b, a) for a, b in pairs] for pairs in (with_next, with_last))
    pay = f32(8, NY, NZ)
    packed = f32(DEV * SLOTS, NZ)
    dma = pltpu.SemaphoreType.DMA
    one_e, two_e = call(
        field_halo_kernel, "field_halo", [HBM], [pay, pay],
        [pltpu.VMEM((NF, 2, 2, NY, NZ), F32), pltpu.VMEM((NF, 2, 3, NY, NZ), F32), dma((2 * NF,))], 400_000, 1_200_000,
    )(fields)
    gone_e = lax.ppermute(one_e, BRICK_AXES, with_next)
    gtwo_e = lax.ppermute(two_e, BRICK_AXES, with_last)
    one_r, two_r = call(
        residual_halo_kernel, "residual_halo", [HBM] * 4, [pay, pay],
        [
            pltpu.SMEM((NF,), F32),
            pltpu.VMEM((NF, 2, 3, 2, NY, NZ), F32),
            pltpu.VMEM((NF, 2, 3, 2, NY, NZ), F32),
            pltpu.VMEM((NF, 2, 2, NY, NZ), F32),
            pltpu.VMEM((NF, 2, 3, NY, NZ), F32),
            pltpu.VMEM((2, NY, NZ), F32),
            dma((11,)),
        ], 2_000_000, 3_000_000,
    )(omegas, fields, sources, conductivity)
    gone_r = lax.ppermute(one_r, BRICK_AXES, with_next)
    gtwo_r = lax.ppermute(two_r, BRICK_AXES, with_last)
    fields_v, sources_v, conductivity_v, _ = lax.optimization_barrier((fields_in, sources_in, conductivity_in, two_r))
    fields_v, sources_v, conductivity_v = (
        pltpu.with_memory_space_constraint(x, pltpu.VMEM) for x in (fields_v, sources_v, conductivity_v)
    )
    halo = [pltpu.VMEM((8, PAD + NY, NZ), F32), pltpu.VMEM((4, NY, NZ), F32)]
    r, slot, index = call(
        residual_kernel, "residual", [SMEM] + [VMEM] * 6,
        [f32(12, PL + 1, NY + PAD, NZ), jax.ShapeDtypeStruct((8, ROWS), I32), f32(DEV, NZ)],
        halo, 30_000_000, 8_000_000,
    )(
        omegas_in, fields_v, sources_v, conductivity_v,
        row_brick.reshape(1, ROWS), row_offset, owner_map.reshape(1, DEV),
    )
    part, rest, fac, _ = pl.pallas_call(
        adjoint_kernel,
        in_specs=[SMEM, SMEM] + [VMEM] * 7,
        out_specs=[VMEM] * 4,
        out_shape=[packed, f32(2, NY, NZ), f32(20, NY, NZ), f32(12, PL + 1, NY + PAD, NZ)],
        input_output_aliases={8: 3},
        scratch_shapes=halo + [pltpu.VMEM((ROWS, NZ), F32)],
        compiler_params=pltpu.CompilerParams(vmem_limit_bytes=LIMIT),
        cost_estimate=pl.CostEstimate(flops=40_000_000, bytes_accessed=8_000_000, transcendentals=0),
        name="adjoint",
    )(omegas_in, tx_bricks, fields_v, conductivity_v, slot, index, gone_e, gtwo_e, r)
    (send,) = call(
        residual_fix_kernel, "residual_fix", [VMEM] * 6, [packed], [pltpu.VMEM((2 * NY, NZ), F32)], 20_000_000, 3_000_000,
    )(fac, rest, gone_r, gtwo_r, slot, part)
    got = lax.all_to_all(send.reshape(DEV, 1, SLOTS * NZ), SWAP_AXES, 0, 0, tiled=True).reshape(DEV * SLOTS, NZ)
    return pl.pallas_call(
        owner_kernel,
        in_specs=[VMEM],
        out_specs=VMEM,
        out_shape=f32(G_DEV, NZ),
        compiler_params=pltpu.CompilerParams(vmem_limit_bytes=LIMIT),
        name="owner_sum",
    )(got)


def solution(mesh):
    grid = Mesh(mesh.devices.reshape(4, 2, 4, 4), ("y", "core", "x", "z"))
    return jax.shard_map(
        per_device,
        mesh=grid,
        in_specs=(
            P(TX_AXES, None, None, None, BRICK_AXES, None, None),
            P(TX_AXES, None, None, None, BRICK_AXES, None, None),
            P(TX_AXES, BRICK_AXES, None, None),
            P(),
            P(),
            P(),
            P(TX_AXES, BRICK_AXES, None),
            P(TX_AXES, BRICK_AXES),
        ),
        out_specs=P(TX_AXES + BRICK_AXES, None),
        check_vma=False,
    )
```

```python
import jax
import jax.numpy as jnp
from jax import lax
from jax.experimental import pallas as pl
from jax.experimental.pallas import tpu as pltpu
from jax.sharding import Mesh, PartitionSpec as P

PL, NY, NZ, NF = 8, 64, 128, 2
ROWS = PL * NY
G_DEV = 32
CAP = 8
DEV = 128
SLOTS = CAP + 1
BRICK = 16
TX_AXES, BRICK_AXES = ("y", "core"), ("x", "z")
SWAP_AXES = ("core", "y", "x", "z")
PAD = 8
CH = 16
F32, BF16, I32 = jnp.float32, jnp.bfloat16, jnp.int32
SCALE = 0.003


def fy(v):
    rows = lax.broadcasted_iota(I32, v.shape, 0)
    return jnp.where(rows == NY - 1, 0.0, pltpu.roll(v, NY - 1, 0)) - v


def by(v):
    rows = lax.broadcasted_iota(I32, v.shape, 0)
    return v - jnp.where(rows == 0, 0.0, pltpu.roll(v, 1, 0))


def fz(v):
    lanes = lax.broadcasted_iota(I32, v.shape, 1)
    return jnp.where(lanes == NZ - 1, 0.0, pltpu.roll(v, NZ - 1, 1)) - v


def bz(v):
    lanes = lax.broadcasted_iota(I32, v.shape, 1)
    return v - jnp.where(lanes == 0, 0.0, pltpu.roll(v, 1, 1))


def q_of(vx, vy, vz):
    return fz(vx) + vz, vy + fy(vx)


def rotate(curl, part, weight, other):
    return curl - weight * other if part == 0 else curl + weight * other


def signed(part, value):
    return value if part == 1 else -value


def odd_brick():
    return (lax.axis_index(BRICK_AXES) & 1) == 1


def field_halo_kernel(e_hbm, one_ref, two_ref, lo_ref, hi_ref, sems):
    odd = odd_brick()
    hi = pltpu.make_async_copy(e_hbm.at[0, :, :, :, PL - 1], hi_ref, sems.at[0])
    lo = pltpu.make_async_copy(e_hbm.at[0, :, :, pl.ds(1, 2), 0], lo_ref, sems.at[1])
    hi.start()
    lo.start()
    hi.wait()
    lo.wait()
    for f in range(NF):
        for part in range(2):
            q = q_of(*(hi_ref[f, part, c] for c in range(3)))
            for c in range(2):
                at = 2 * (2 * f + part) + c
                one_ref[at] = jnp.where(odd, q[c], lo_ref[f, part, c])
                two_ref[at] = jnp.where(odd, lo_ref[f, part, c], q[c])


def one_hot(cond):
    return jnp.where(cond, 1.0, 0.0).astype(BF16)


def dot(a, b):
    return jnp.dot(a, b, preferred_element_type=F32)


def row_slots(rb_ref, ro_ref, own_ref, slot_ref, index_ref):
    bt = lax.broadcasted_iota(I32, (DEV, ROWS), 0) == rb_ref[...]
    hot = one_hot(bt)
    before = one_hot(lax.broadcasted_iota(I32, (ROWS, ROWS), 0) < lax.broadcasted_iota(I32, (ROWS, ROWS), 1))
    counts = dot(hot, before)
    rank = jnp.sum(jnp.where(bt, counts, 0.0), axis=0, keepdims=True)
    own8 = jnp.broadcast_to(own_ref[...].astype(F32), (8, DEV)).astype(BF16)
    dest = dot(own8, hot)[0:1].astype(I32)
    dest = (dest & 3) * 1 + ((dest >> 2) & 3) * 4 + (dest >> 5) * 16 + ((dest >> 4) & 1) * 64
    rank = rank.astype(I32)
    slot = dest * SLOTS + rank
    slot_ref[...] = jnp.broadcast_to(slot, (8, ROWS))
    codes = jnp.where(lax.broadcasted_iota(I32, (NZ, ROWS), 0) == rank, (ro_ref[...] + 1).astype(F32), 0.0).astype(BF16)
    mine = one_hot(lax.broadcasted_iota(I32, (DEV, ROWS), 0) == dest)
    index_ref[...] = lax.dot_general(mine, codes, (((1,), (1,)), ((), ())), preferred_element_type=F32)


def residual_halo_kernel(
    om_hbm, e_hbm, s_hbm, c_hbm, rb_hbm, ro_hbm, own_hbm, one_ref, two_ref, slot_ref, index_ref,
    om_ref, rb_ref, ro_ref, own_ref, elo_ref, ehi_ref, slo_ref, shi_ref, cc_ref, sems,
):
    odd = odd_brick()
    few = [
        pltpu.make_async_copy(rb_hbm, rb_ref, sems.at[8]),
        pltpu.make_async_copy(ro_hbm, ro_ref, sems.at[9]),
        pltpu.make_async_copy(own_hbm, own_ref, sems.at[10]),
        pltpu.make_async_copy(om_hbm, om_ref, sems.at[11]),
        pltpu.make_async_copy(c_hbm.at[0, 0], cc_ref.at[0], sems.at[12]),
        pltpu.make_async_copy(c_hbm.at[0, PL - 1], cc_ref.at[1], sems.at[13]),
    ]
    big = [
        [
            pltpu.make_async_copy(e_hbm.at[0, f, :, :, pl.ds(PL - 2, 2)], ehi_ref.at[f], sems.at[4 * f]),
            pltpu.make_async_copy(s_hbm.at[0, f, :, :, PL - 1], shi_ref.at[f], sems.at[4 * f + 1]),
            pltpu.make_async_copy(e_hbm.at[0, f, :, :, pl.ds(0, 2)], elo_ref.at[f], sems.at[4 * f + 2]),
            pltpu.make_async_copy(s_hbm.at[0, f, :, pl.ds(1, 2), 0], slo_ref.at[f], sems.at[4 * f + 3]),
        ]
        for f in range(NF)
    ]
    for copy in few + big[0] + big[1]:
        copy.start()
    for copy in few:
        copy.wait()
    row_slots(rb_ref, ro_ref, own_ref, slot_ref, index_ref)
    for f in range(NF):
        om = om_ref[f]
        big[f][0].wait()
        big[f][1].wait()
        for part in range(2):
            ch = 2 * f + part
            ux, uy, uz = (ehi_ref[f, part, c, 0] for c in range(3))
            vx, vy, vz = (ehi_ref[f, part, c, 1] for c in range(3))
            hy, qz = q_of(vx, vy, vz)
            hz = -qz
            hx = fy(vz) - fz(vy)
            gy = fz(ux) - (vz - uz)
            gz = (vy - uy) - fy(ux)
            w = om * cc_ref[1]
            o = [ehi_ref[f, 1 - part, c, 1] for c in range(3)]
            rx = rotate(by(hz) - bz(hy), part, w, o[0]) - shi_ref[f, part, 0]
            ry = rotate(bz(hx) - (hz - gz), part, w, o[1]) - shi_ref[f, part, 1]
            rz = rotate((hy - gy) - by(hx), part, w, o[2]) - shi_ref[f, part, 2]
            one_ref[2 * ch], one_ref[2 * ch + 1] = q_of(rx, ry, rz)
        big[f][2].wait()
        big[f][3].wait()
        for part in range(2):
            ch = 2 * f + part
            vx, vy, vz = (elo_ref[f, part, c, 0] for c in range(3))
            hx = fy(vz) - fz(vy)
            hy = fz(vx) - (elo_ref[f, part, 2, 1] - vz)
            hz = (elo_ref[f, part, 1, 1] - vy) - fy(vx)
            w = om * cc_ref[0]
            dn = [
                rotate(bz(hx) - hz, part, w, elo_ref[f, 1 - part, 1, 0]) - slo_ref[f, part, 0],
                rotate(hy - by(hx), part, w, elo_ref[f, 1 - part, 2, 0]) - slo_ref[f, part, 1],
            ]
            for c in range(2):
                up = one_ref[2 * ch + c]
                one_ref[2 * ch + c] = jnp.where(odd, up, dn[c])
                two_ref[2 * ch + c] = jnp.where(odd, dn[c], up)


def pick(hot, v):
    hi = v.astype(BF16)
    low = (v - hi.astype(F32)).astype(BF16)
    both = dot(hot, jnp.concatenate([hi, low], axis=1))
    return both[:, 0:NZ] + both[:, NZ:2 * NZ]


def place(tb_ref):
    brick = lax.axis_index(BRICK_AXES)
    span = tb_ref[lax.axis_index(TX_AXES)]
    live = jnp.where(brick < span, 1.0, 0.0).astype(F32)
    low = jnp.where(brick > 0, 1.0, 0.0).astype(F32)
    nxt = jnp.where(brick + 1 < span, 1.0, 0.0).astype(F32)
    return live, low, nxt


def curl(get, h_ref, g_ref, p, y, ch):
    lanes = lax.broadcasted_iota(I32, (CH, NZ), 1)

    def nz_(v):
        return jnp.where(lanes == NZ - 1, 0.0, pltpu.roll(v, NZ - 1, 1))

    def pz_(v):
        return jnp.where(lanes == 0, 0.0, pltpu.roll(v, 1, 1))

    vx, vy, vz = (get(c, p, y) for c in range(3))
    hx = (get(2, p, y + 1) - vz) - (nz_(vy) - vy)
    hy = (nz_(vx) - vx) - (get(2, p + 1, y) - vz)
    hz = (get(1, p + 1, y) - vy) - (get(0, p, y + 1) - vx)
    gy = g_ref[ch, y:y + CH]
    gz = h_ref[2 * ch + 1, PAD + y:PAD + y + CH]
    h_ref[2 * ch, PAD + y:PAD + y + CH] = hx
    h_ref[2 * ch + 1, PAD + y:PAD + y + CH] = hz
    g_ref[ch, y:y + CH] = hy
    hxp = h_ref[2 * ch, PAD + y - 1:PAD + y - 1 + CH]
    hzp = h_ref[2 * ch + 1, PAD + y - 1:PAD + y - 1 + CH]
    cx = (hz - hzp) - (hy - pz_(hy))
    cy = (hx - pz_(hx)) - (hz - gz)
    cz = (hy - gy) - (hx - hxp)
    return (vx, vy, vz), (cx, cy, cz)


def residual_kernel(om_ref, e_ref, s_ref, c_ref, r_ref, h_ref, g_ref):
    zero = jnp.zeros((NY, NZ), F32)
    zpad = jnp.zeros((PAD, NZ), F32)
    for i in range(12):
        for p in range(PL):
            r_ref[i, p, NY:NY + PAD] = zpad
    for i in range(8):
        h_ref[i, 0:PAD] = zpad
        h_ref[i, PAD:PAD + NY] = zero
    for i in range(4):
        g_ref[i] = zero

    rows = lax.broadcasted_iota(I32, (CH, NZ), 0)

    def step(p, carry):
        after = jnp.minimum(p + 1, PL - 1)
        inside = jnp.where(p < PL - 1, 1.0, 0.0).astype(F32)
        for y in range(0, NY, CH):
            sig = c_ref[0, p, y:y + CH]
            for f in range(NF):
                w = om_ref[f] * sig
                for part in range(2):
                    ch = 2 * f + part

                    def get(c, q, r):
                        if q is not p:
                            return e_ref[0, f, part, c, after, r:r + CH] * inside
                        if r + CH <= NY:
                            return e_ref[0, f, part, c, p, r:r + CH]
                        last = e_ref[0, f, part, c, p, NY - CH:NY]
                        return jnp.where(rows == CH - 1, 0.0, pltpu.roll(last, CH - 1, 0))

                    _, cs = curl(get, h_ref, g_ref, p, y, ch)
                    for c in range(3):
                        o = e_ref[0, f, 1 - part, c, p, y:y + CH]
                        r_ref[3 * ch + c, p, y:y + CH] = rotate(cs[c], part, w, o) - s_ref[0, f, part, c, p, y:y + CH]
        return carry

    lax.fori_loop(0, PL, step, 0)
    for ch in range(4):
        r_ref[3 * ch + 1, PL, 0:NY] = h_ref[2 * ch + 1, PAD:PAD + NY]
        r_ref[3 * ch + 2, PL, 0:NY] = -g_ref[ch]


def adjoint_kernel(
    om_ref, tb_ref, e_ref, c_ref, slot_ref, index_ref, gone_ref, gtwo_ref, rin_ref,
    part_ref, rest_ref, fac_ref, r_ref, h_ref, g_ref, loc_ref,
):
    live, low, nxt = place(tb_ref)
    odd = odd_brick()
    end = PL - 1
    zpad = jnp.zeros((PAD, NZ), F32)
    for i in range(8):
        h_ref[i, 0:PAD] = zpad
    for f in range(NF):
        weight = SCALE * om_ref[f] * live
        for part in range(2):
            ch = 2 * f + part
            x, y, z = 3 * ch, 3 * ch + 1, 3 * ch + 2
            ey, ez = e_ref[0, f, part, 1, 0], e_ref[0, f, part, 2, 0]
            first = [gone_ref[2 * ch + c] for c in range(2)]
            second = [gtwo_ref[2 * ch + c] for c in range(2)]
            qy, qz = (jnp.where(odd, second[c], first[c]) for c in range(2))
            ry = rin_ref[y, 0, 0:NY] + low * (ey - qz)
            rz = rin_ref[z, 0, 0:NY] + low * (ez - qy)
            r_ref[y, 0, 0:NY] = ry
            r_ref[z, 0, 0:NY] = rz
            div = by(ey) + bz(ez)
            g_ref[ch] = low * (fz(div) - ez - rz)
            h_ref[2 * ch + 1, PAD:PAD + NY] = low * (ry - fy(div) + ey)
            ey, ez = (nxt * jnp.where(odd, first[c], second[c]) for c in range(2))
            r_ref[x, end, 0:NY] = rin_ref[x, end, 0:NY] + (by(ey) + bz(ez))
            r_ref[y, end, 0:NY] = rin_ref[y, end, 0:NY] - ey
            r_ref[z, end, 0:NY] = rin_ref[z, end, 0:NY] - ez
            r_ref[y, PL, 0:NY] = nxt * rin_ref[y, PL, 0:NY] + ey
            r_ref[z, PL, 0:NY] = nxt * rin_ref[z, PL, 0:NY] + ez
            scale = -signed(part, weight) * low
            fac_ref[2 * ch] = scale * e_ref[0, f, 1 - part, 2, 0]
            fac_ref[2 * ch + 1] = scale * e_ref[0, f, 1 - part, 1, 0]
            scale = signed(part, weight) * nxt
            for c in range(3):
                fac_ref[8 + 3 * ch + c] = scale * e_ref[0, f, 1 - part, c, end]

    def step(p, carry):
        for y in range(0, NY, CH):
            sig = c_ref[0, p, y:y + CH]
            acc = jnp.zeros((CH, NZ), F32)
            for f in range(NF):
                om = om_ref[f]
                tot = jnp.zeros((CH, NZ), F32)
                dia = jnp.zeros((CH, NZ), F32)
                for part in range(2):
                    ch = 2 * f + part
                    vs, cs = curl(lambda c, q, r: r_ref[3 * ch + c, q, r:r + CH], h_ref, g_ref, p, y, ch)
                    o = [e_ref[0, f, 1 - part, c, p, y:y + CH] for c in range(3)]
                    s = [e_ref[0, f, part, c, p, y:y + CH] for c in range(3)]
                    tot = tot + signed(part, o[0] * cs[0] + o[1] * cs[1] + o[2] * cs[2])
                    dia = dia + (s[0] * vs[0] + s[1] * vs[1] + s[2] * vs[2])
                acc = acc + (SCALE * om * live) * (tot + (om * sig) * dia)
            loc_ref[pl.ds(pl.multiple_of(p * NY + y, CH), CH), :] = acc
        return carry

    lax.fori_loop(0, PL, step, 0)

    rest_ref[0] = loc_ref[0:NY]
    rest_ref[1] = loc_ref[ROWS - NY:ROWS]
    lo, hi = NY, ROWS - NY
    at = lax.broadcasted_iota(I32, (DEV * SLOTS, hi - lo), 0)
    part_ref[...] = pick(one_hot(at == slot_ref[0:1, lo:hi]), loc_ref[lo:hi])
    part_ref[pl.ds(CAP, DEV, stride=SLOTS), :] = index_ref[...]


def residual_fix_kernel(fac_ref, rest_ref, gone_ref, gtwo_ref, slot_ref, part_ref, out_ref, two_ref):
    odd = odd_brick()
    low, high = rest_ref[0], rest_ref[1]
    for ch in range(4):
        first = [gone_ref[2 * ch + c] for c in range(2)]
        second = [gtwo_ref[2 * ch + c] for c in range(2)]
        qy, qz = (jnp.where(odd, second[c], first[c]) for c in range(2))
        ry, rz = (jnp.where(odd, first[c], second[c]) for c in range(2))
        low = low + (fac_ref[2 * ch] * qy + fac_ref[2 * ch + 1] * qz)
        o = [fac_ref[8 + 3 * ch + c] for c in range(3)]
        high = high + (o[0] * (by(ry) + bz(rz)) - o[1] * ry - o[2] * rz)
    two_ref[0:NY] = low
    two_ref[NY:2 * NY] = high
    at = lax.broadcasted_iota(I32, (DEV * SLOTS, NY), 0)
    hot = jnp.concatenate([one_hot(at == slot_ref[0:1, 0:NY]), one_hot(at == slot_ref[0:1, ROWS - NY:ROWS])], axis=1)
    out_ref[...] = part_ref[...] + pick(hot, two_ref[...])


def owner_kernel(got_ref, out_ref):
    codes = got_ref[pl.ds(CAP, DEV, stride=SLOTS), :]
    offs = codes.T[0:CAP].astype(I32)
    want = lax.broadcasted_iota(I32, (G_DEV, DEV), 0) + 1
    hot = jnp.concatenate([one_hot(want == offs[k:k + 1]) for k in range(CAP)], axis=1)
    out_ref[...] = pick(hot, jnp.concatenate([got_ref[pl.ds(k, DEV, stride=SLOTS), :] for k in range(CAP)], axis=0))


SMEM = pl.BlockSpec(memory_space=pltpu.SMEM)
VMEM = pl.BlockSpec(memory_space=pltpu.VMEM)
HBM = pl.BlockSpec(memory_space=pltpu.HBM)
LIMIT = 40 * 1024 * 1024


def f32(*shape):
    return jax.ShapeDtypeStruct(shape, F32)


def call(kernel, name, ins, outs, scratch, flops, moved):
    return pl.pallas_call(
        kernel,
        in_specs=ins,
        out_specs=[VMEM] * len(outs),
        out_shape=outs,
        scratch_shapes=scratch,
        compiler_params=pltpu.CompilerParams(vmem_limit_bytes=LIMIT),
        cost_estimate=pl.CostEstimate(flops=flops, bytes_accessed=moved, transcendentals=0),
        name=name,
    )


def per_device(fields, sources, conductivity, omegas, tx_bricks, owner_map, row_brick, row_offset):
    fields_in, sources_in, conductivity_in, omegas_in = fields, sources, conductivity, omegas
    fields, sources, conductivity, omegas = (
        pltpu.with_memory_space_constraint(x, pltpu.HBM) for x in (fields, sources, conductivity, omegas)
    )
    with_next = [(i, (i + 1) % BRICK) for i in range(1, BRICK, 2)]
    with_last = [(i, i + 1) for i in range(0, BRICK, 2)]
    with_next, with_last = (pairs + [(b, a) for a, b in pairs] for pairs in (with_next, with_last))
    pay = f32(8, NY, NZ)
    packed = f32(DEV * SLOTS, NZ)
    dma = pltpu.SemaphoreType.DMA
    one_e, two_e = call(
        field_halo_kernel, "field_halo", [HBM], [pay, pay],
        [pltpu.VMEM((NF, 2, 2, NY, NZ), F32), pltpu.VMEM((NF, 2, 3, NY, NZ), F32), dma((2 * NF,))], 400_000, 1_200_000,
    )(fields)
    gone_e = lax.ppermute(one_e, BRICK_AXES, with_next)
    gtwo_e = lax.ppermute(two_e, BRICK_AXES, with_last)
    one_r, two_r, slot, index = call(
        residual_halo_kernel, "residual_halo", [HBM] * 7,
        [pay, pay, jax.ShapeDtypeStruct((8, ROWS), I32), f32(DEV, NZ)],
        [
            pltpu.SMEM((NF,), F32),
            pltpu.VMEM((1, ROWS), I32),
            pltpu.VMEM((1, ROWS), I32),
            pltpu.VMEM((1, DEV), I32),
            pltpu.VMEM((NF, 2, 3, 2, NY, NZ), F32),
            pltpu.VMEM((NF, 2, 3, 2, NY, NZ), F32),
            pltpu.VMEM((NF, 2, 2, NY, NZ), F32),
            pltpu.VMEM((NF, 2, 3, NY, NZ), F32),
            pltpu.VMEM((2, NY, NZ), F32),
            dma((14,)),
        ], 2_000_000, 3_000_000,
    )(
        omegas, fields, sources, conductivity,
        *(
            pltpu.with_memory_space_constraint(x, pltpu.HBM)
            for x in (row_brick.reshape(1, ROWS), row_offset, owner_map.reshape(1, DEV))
        ),
    )
    gone_r = lax.ppermute(one_r, BRICK_AXES, with_next)
    gtwo_r = lax.ppermute(two_r, BRICK_AXES, with_last)
    fields_v, sources_v, conductivity_v, _ = lax.optimization_barrier((fields_in, sources_in, conductivity_in, two_r))
    fields_v, sources_v, conductivity_v = (
        pltpu.with_memory_space_constraint(x, pltpu.VMEM) for x in (fields_v, sources_v, conductivity_v)
    )
    halo = [pltpu.VMEM((8, PAD + NY, NZ), F32), pltpu.VMEM((4, NY, NZ), F32)]
    (r,) = call(
        residual_kernel, "residual", [SMEM] + [VMEM] * 3, [f32(12, PL + 1, NY + PAD, NZ)], halo, 30_000_000, 8_000_000,
    )(omegas_in, fields_v, sources_v, conductivity_v)
    part, rest, fac, _ = pl.pallas_call(
        adjoint_kernel,
        in_specs=[SMEM, SMEM] + [VMEM] * 7,
        out_specs=[VMEM] * 4,
        out_shape=[packed, f32(2, NY, NZ), f32(20, NY, NZ), f32(12, PL + 1, NY + PAD, NZ)],
        input_output_aliases={8: 3},
        scratch_shapes=halo + [pltpu.VMEM((ROWS, NZ), F32)],
        compiler_params=pltpu.CompilerParams(vmem_limit_bytes=LIMIT),
        cost_estimate=pl.CostEstimate(flops=40_000_000, bytes_accessed=8_000_000, transcendentals=0),
        name="adjoint",
    )(omegas_in, tx_bricks, fields_v, conductivity_v, slot, index, gone_e, gtwo_e, r)
    (send,) = call(
        residual_fix_kernel, "residual_fix", [VMEM] * 6, [packed], [pltpu.VMEM((2 * NY, NZ), F32)], 20_000_000, 3_000_000,
    )(fac, rest, gone_r, gtwo_r, slot, part)
    got = lax.all_to_all(send.reshape(DEV, 1, SLOTS * NZ), SWAP_AXES, 0, 0, tiled=True).reshape(DEV * SLOTS, NZ)
    return pl.pallas_call(
        owner_kernel,
        in_specs=[VMEM],
        out_specs=VMEM,
        out_shape=f32(G_DEV, NZ),
        compiler_params=pltpu.CompilerParams(vmem_limit_bytes=LIMIT),
        name="owner_sum",
    )(got)


def solution(mesh):
    grid = Mesh(mesh.devices.reshape(4, 2, 4, 4), ("y", "core", "x", "z"))
    return jax.shard_map(
        per_device,
        mesh=grid,
        in_specs=(
            P(TX_AXES, None, None, None, BRICK_AXES, None, None),
            P(TX_AXES, None, None, None, BRICK_AXES, None, None),
            P(TX_AXES, BRICK_AXES, None, None),
            P(),
            P(),
            P(),
            P(TX_AXES, BRICK_AXES, None),
            P(TX_AXES, BRICK_AXES),
        ),
        out_specs=P(TX_AXES + BRICK_AXES, None),
        check_vma=False,
    )
```

```python
import jax
import jax.numpy as jnp
from jax import lax
from jax.experimental import pallas as pl
from jax.experimental.pallas import tpu as pltpu
from jax.sharding import Mesh, PartitionSpec as P

PL, NY, NZ, NF = 8, 64, 128, 2
ROWS = PL * NY
G_DEV = 32
CAP = 8
DEV = 128
SLOTS = CAP + 1
BRICK = 16
TX_AXES, BRICK_AXES = ("y", "core"), ("x", "z")
SWAP_AXES = ("core", "y", "x", "z")
PAD = 8
CH = 16
F32, BF16, I32 = jnp.float32, jnp.bfloat16, jnp.int32
SCALE = 0.003


def fy(v):
    rows = lax.broadcasted_iota(I32, v.shape, 0)
    return jnp.where(rows == NY - 1, 0.0, pltpu.roll(v, NY - 1, 0)) - v


def by(v):
    rows = lax.broadcasted_iota(I32, v.shape, 0)
    return v - jnp.where(rows == 0, 0.0, pltpu.roll(v, 1, 0))


def fz(v):
    lanes = lax.broadcasted_iota(I32, v.shape, 1)
    return jnp.where(lanes == NZ - 1, 0.0, pltpu.roll(v, NZ - 1, 1)) - v


def bz(v):
    lanes = lax.broadcasted_iota(I32, v.shape, 1)
    return v - jnp.where(lanes == 0, 0.0, pltpu.roll(v, 1, 1))


def q_of(vx, vy, vz):
    return fz(vx) + vz, vy + fy(vx)


def rotate(curl, part, weight, other):
    return curl - weight * other if part == 0 else curl + weight * other


def signed(part, value):
    return value if part == 1 else -value


def odd_brick():
    return (lax.axis_index(BRICK_AXES) & 1) == 1


def field_halo_kernel(e_hbm, one_ref, two_ref, lo_ref, hi_ref, sems):
    odd = odd_brick()
    hi = pltpu.make_async_copy(e_hbm.at[0, :, :, :, PL - 1], hi_ref, sems.at[0])
    lo = pltpu.make_async_copy(e_hbm.at[0, :, :, pl.ds(1, 2), 0], lo_ref, sems.at[1])
    hi.start()
    lo.start()
    hi.wait()
    lo.wait()
    for f in range(NF):
        for part in range(2):
            q = q_of(*(hi_ref[f, part, c] for c in range(3)))
            for c in range(2):
                at = 2 * (2 * f + part) + c
                one_ref[at] = jnp.where(odd, q[c], lo_ref[f, part, c])
                two_ref[at] = jnp.where(odd, lo_ref[f, part, c], q[c])


def one_hot(cond):
    return jnp.where(cond, 1.0, 0.0).astype(BF16)


def dot(a, b):
    return jnp.dot(a, b, preferred_element_type=F32)


def row_slots(rb_ref, ro_ref, own_ref, slot_ref, index_ref):
    bt = lax.broadcasted_iota(I32, (DEV, ROWS), 0) == rb_ref[...]
    hot = one_hot(bt)
    before = one_hot(lax.broadcasted_iota(I32, (ROWS, ROWS), 0) < lax.broadcasted_iota(I32, (ROWS, ROWS), 1))
    counts = dot(hot, before)
    rank = jnp.sum(jnp.where(bt, counts, 0.0), axis=0, keepdims=True)
    own8 = jnp.broadcast_to(own_ref[...].astype(F32), (8, DEV)).astype(BF16)
    dest = dot(own8, hot)[0:1].astype(I32)
    dest = (dest & 3) * 1 + ((dest >> 2) & 3) * 4 + (dest >> 5) * 16 + ((dest >> 4) & 1) * 64
    rank = rank.astype(I32)
    slot = dest * SLOTS + rank
    slot_ref[...] = jnp.broadcast_to(slot, (8, ROWS))
    codes = jnp.where(lax.broadcasted_iota(I32, (NZ, ROWS), 0) == rank, (ro_ref[...] + 1).astype(F32), 0.0).astype(BF16)
    mine = one_hot(lax.broadcasted_iota(I32, (DEV, ROWS), 0) == dest)
    index_ref[...] = lax.dot_general(mine, codes, (((1,), (1,)), ((), ())), preferred_element_type=F32)


def residual_halo_kernel(
    om_hbm, e_hbm, s_hbm, c_hbm, rb_hbm, ro_hbm, own_hbm, one_ref, two_ref, slot_ref, index_ref,
    om_ref, rb_ref, ro_ref, own_ref, elo_ref, ehi_ref, slo_ref, shi_ref, cc_ref, sems,
):
    odd = odd_brick()
    few = [
        pltpu.make_async_copy(rb_hbm, rb_ref, sems.at[8]),
        pltpu.make_async_copy(ro_hbm, ro_ref, sems.at[9]),
        pltpu.make_async_copy(own_hbm, own_ref, sems.at[10]),
        pltpu.make_async_copy(om_hbm, om_ref, sems.at[11]),
        pltpu.make_async_copy(c_hbm.at[0, 0], cc_ref.at[0], sems.at[12]),
        pltpu.make_async_copy(c_hbm.at[0, PL - 1], cc_ref.at[1], sems.at[13]),
    ]
    big = [
        [
            pltpu.make_async_copy(e_hbm.at[0, f, :, :, pl.ds(PL - 2, 2)], ehi_ref.at[f], sems.at[4 * f]),
            pltpu.make_async_copy(s_hbm.at[0, f, :, :, PL - 1], shi_ref.at[f], sems.at[4 * f + 1]),
            pltpu.make_async_copy(e_hbm.at[0, f, :, :, pl.ds(0, 2)], elo_ref.at[f], sems.at[4 * f + 2]),
            pltpu.make_async_copy(s_hbm.at[0, f, :, pl.ds(1, 2), 0], slo_ref.at[f], sems.at[4 * f + 3]),
        ]
        for f in range(NF)
    ]
    for copy in few + big[0] + big[1]:
        copy.start()
    for copy in few:
        copy.wait()
    row_slots(rb_ref, ro_ref, own_ref, slot_ref, index_ref)
    for f in range(NF):
        om = om_ref[f]
        big[f][0].wait()
        big[f][1].wait()
        for part in range(2):
            ch = 2 * f + part
            ux, uy, uz = (ehi_ref[f, part, c, 0] for c in range(3))
            vx, vy, vz = (ehi_ref[f, part, c, 1] for c in range(3))
            hy, qz = q_of(vx, vy, vz)
            hz = -qz
            hx = fy(vz) - fz(vy)
            gy = fz(ux) - (vz - uz)
            gz = (vy - uy) - fy(ux)
            w = om * cc_ref[1]
            o = [ehi_ref[f, 1 - part, c, 1] for c in range(3)]
            rx = rotate(by(hz) - bz(hy), part, w, o[0]) - shi_ref[f, part, 0]
            ry = rotate(bz(hx) - (hz - gz), part, w, o[1]) - shi_ref[f, part, 1]
            rz = rotate((hy - gy) - by(hx), part, w, o[2]) - shi_ref[f, part, 2]
            one_ref[2 * ch], one_ref[2 * ch + 1] = q_of(rx, ry, rz)
        big[f][2].wait()
        big[f][3].wait()
        for part in range(2):
            ch = 2 * f + part
            vx, vy, vz = (elo_ref[f, part, c, 0] for c in range(3))
            hx = fy(vz) - fz(vy)
            hy = fz(vx) - (elo_ref[f, part, 2, 1] - vz)
            hz = (elo_ref[f, part, 1, 1] - vy) - fy(vx)
            w = om * cc_ref[0]
            dn = [
                rotate(bz(hx) - hz, part, w, elo_ref[f, 1 - part, 1, 0]) - slo_ref[f, part, 0],
                rotate(hy - by(hx), part, w, elo_ref[f, 1 - part, 2, 0]) - slo_ref[f, part, 1],
            ]
            for c in range(2):
                up = one_ref[2 * ch + c]
                one_ref[2 * ch + c] = jnp.where(odd, up, dn[c])
                two_ref[2 * ch + c] = jnp.where(odd, dn[c], up)


def pick(hot, v):
    hi = v.astype(BF16)
    low = (v - hi.astype(F32)).astype(BF16)
    both = dot(hot, jnp.concatenate([hi, low], axis=1))
    return both[:, 0:NZ] + both[:, NZ:2 * NZ]


def place(tb_ref):
    brick = lax.axis_index(BRICK_AXES)
    span = tb_ref[lax.axis_index(TX_AXES)]
    live = jnp.where(brick < span, 1.0, 0.0).astype(F32)
    low = jnp.where(brick > 0, 1.0, 0.0).astype(F32)
    nxt = jnp.where(brick + 1 < span, 1.0, 0.0).astype(F32)
    return live, low, nxt


def curl(get, h_ref, g_ref, p, y, ch):
    lanes = lax.broadcasted_iota(I32, (CH, NZ), 1)

    def nz_(v):
        return jnp.where(lanes == NZ - 1, 0.0, pltpu.roll(v, NZ - 1, 1))

    def pz_(v):
        return jnp.where(lanes == 0, 0.0, pltpu.roll(v, 1, 1))

    vx, vy, vz = (get(c, p, y) for c in range(3))
    hx = (get(2, p, y + 1) - vz) - (nz_(vy) - vy)
    hy = (nz_(vx) - vx) - (get(2, p + 1, y) - vz)
    hz = (get(1, p + 1, y) - vy) - (get(0, p, y + 1) - vx)
    gy = g_ref[ch, y:y + CH]
    gz = h_ref[2 * ch + 1, PAD + y:PAD + y + CH]
    h_ref[2 * ch, PAD + y:PAD + y + CH] = hx
    h_ref[2 * ch + 1, PAD + y:PAD + y + CH] = hz
    g_ref[ch, y:y + CH] = hy
    hxp = h_ref[2 * ch, PAD + y - 1:PAD + y - 1 + CH]
    hzp = h_ref[2 * ch + 1, PAD + y - 1:PAD + y - 1 + CH]
    cx = (hz - hzp) - (hy - pz_(hy))
    cy = (hx - pz_(hx)) - (hz - gz)
    cz = (hy - gy) - (hx - hxp)
    return (vx, vy, vz), (cx, cy, cz)


def residual_kernel(om_ref, e_ref, s_ref, c_ref, r_ref, h_ref, g_ref):
    zero = jnp.zeros((NY, NZ), F32)
    zpad = jnp.zeros((PAD, NZ), F32)
    for i in range(12):
        for p in range(PL):
            r_ref[i, p, NY:NY + PAD] = zpad
    for i in range(8):
        h_ref[i, 0:PAD] = zpad
        h_ref[i, PAD:PAD + NY] = zero
    for i in range(4):
        g_ref[i] = zero

    rows = lax.broadcasted_iota(I32, (CH, NZ), 0)

    def step(p, carry):
        after = jnp.minimum(p + 1, PL - 1)
        inside = jnp.where(p < PL - 1, 1.0, 0.0).astype(F32)
        for y in range(0, NY, CH):
            sig = c_ref[0, p, y:y + CH]
            for f in range(NF):
                w = om_ref[f] * sig
                for part in range(2):
                    ch = 2 * f + part

                    def get(c, q, r):
                        if q is not p:
                            return e_ref[0, f, part, c, after, r:r + CH] * inside
                        if r + CH <= NY:
                            return e_ref[0, f, part, c, p, r:r + CH]
                        last = e_ref[0, f, part, c, p, NY - CH:NY]
                        return jnp.where(rows == CH - 1, 0.0, pltpu.roll(last, CH - 1, 0))

                    _, cs = curl(get, h_ref, g_ref, p, y, ch)
                    for c in range(3):
                        o = e_ref[0, f, 1 - part, c, p, y:y + CH]
                        r_ref[3 * ch + c, p, y:y + CH] = rotate(cs[c], part, w, o) - s_ref[0, f, part, c, p, y:y + CH]
        return carry

    lax.fori_loop(0, PL, step, 0)
    for ch in range(4):
        r_ref[3 * ch + 1, PL, 0:NY] = h_ref[2 * ch + 1, PAD:PAD + NY]
        r_ref[3 * ch + 2, PL, 0:NY] = -g_ref[ch]


def adjoint_kernel(
    om_ref, tb_ref, e_ref, c_ref, slot_ref, index_ref, gone_ref, gtwo_ref, rin_ref,
    part_ref, rest_ref, fac_ref, hot_ref, r_ref, h_ref, g_ref, loc_ref,
):
    live, low, nxt = place(tb_ref)
    odd = odd_brick()
    end = PL - 1
    zpad = jnp.zeros((PAD, NZ), F32)
    for i in range(8):
        h_ref[i, 0:PAD] = zpad
    for f in range(NF):
        weight = SCALE * om_ref[f] * live
        for part in range(2):
            ch = 2 * f + part
            x, y, z = 3 * ch, 3 * ch + 1, 3 * ch + 2
            ey, ez = e_ref[0, f, part, 1, 0], e_ref[0, f, part, 2, 0]
            first = [gone_ref[2 * ch + c] for c in range(2)]
            second = [gtwo_ref[2 * ch + c] for c in range(2)]
            qy, qz = (jnp.where(odd, second[c], first[c]) for c in range(2))
            ry = rin_ref[y, 0, 0:NY] + low * (ey - qz)
            rz = rin_ref[z, 0, 0:NY] + low * (ez - qy)
            r_ref[y, 0, 0:NY] = ry
            r_ref[z, 0, 0:NY] = rz
            div = by(ey) + bz(ez)
            g_ref[ch] = low * (fz(div) - ez - rz)
            h_ref[2 * ch + 1, PAD:PAD + NY] = low * (ry - fy(div) + ey)
            ey, ez = (nxt * jnp.where(odd, first[c], second[c]) for c in range(2))
            r_ref[x, end, 0:NY] = rin_ref[x, end, 0:NY] + (by(ey) + bz(ez))
            r_ref[y, end, 0:NY] = rin_ref[y, end, 0:NY] - ey
            r_ref[z, end, 0:NY] = rin_ref[z, end, 0:NY] - ez
            r_ref[y, PL, 0:NY] = nxt * rin_ref[y, PL, 0:NY] + ey
            r_ref[z, PL, 0:NY] = nxt * rin_ref[z, PL, 0:NY] + ez
            scale = -signed(part, weight) * low
            fac_ref[2 * ch] = scale * e_ref[0, f, 1 - part, 2, 0]
            fac_ref[2 * ch + 1] = scale * e_ref[0, f, 1 - part, 1, 0]
            scale = signed(part, weight) * nxt
            for c in range(3):
                fac_ref[8 + 3 * ch + c] = scale * e_ref[0, f, 1 - part, c, end]

    def step(p, carry):
        for y in range(0, NY, CH):
            sig = c_ref[0, p, y:y + CH]
            acc = jnp.zeros((CH, NZ), F32)
            for f in range(NF):
                om = om_ref[f]
                tot = jnp.zeros((CH, NZ), F32)
                dia = jnp.zeros((CH, NZ), F32)
                for part in range(2):
                    ch = 2 * f + part
                    vs, cs = curl(lambda c, q, r: r_ref[3 * ch + c, q, r:r + CH], h_ref, g_ref, p, y, ch)
                    o = [e_ref[0, f, 1 - part, c, p, y:y + CH] for c in range(3)]
                    s = [e_ref[0, f, part, c, p, y:y + CH] for c in range(3)]
                    tot = tot + signed(part, o[0] * cs[0] + o[1] * cs[1] + o[2] * cs[2])
                    dia = dia + (s[0] * vs[0] + s[1] * vs[1] + s[2] * vs[2])
                acc = acc + (SCALE * om * live) * (tot + (om * sig) * dia)
            loc_ref[pl.ds(pl.multiple_of(p * NY + y, CH), CH), :] = acc
        return carry

    lax.fori_loop(0, PL, step, 0)

    ends = lax.broadcasted_iota(I32, (DEV * SLOTS, NY), 0)
    hot_ref[...] = jnp.concatenate(
        [one_hot(ends == slot_ref[0:1, 0:NY]), one_hot(ends == slot_ref[0:1, ROWS - NY:ROWS])], axis=1
    )
    rest_ref[0] = loc_ref[0:NY]
    rest_ref[1] = loc_ref[ROWS - NY:ROWS]
    lo, hi = NY, ROWS - NY
    at = lax.broadcasted_iota(I32, (DEV * SLOTS, hi - lo), 0)
    part_ref[...] = pick(one_hot(at == slot_ref[0:1, lo:hi]), loc_ref[lo:hi])
    part_ref[pl.ds(CAP, DEV, stride=SLOTS), :] = index_ref[...]


def residual_fix_kernel(fac_ref, rest_ref, gone_ref, gtwo_ref, hot_ref, part_ref, out_ref, two_ref):
    odd = odd_brick()
    low, high = rest_ref[0], rest_ref[1]
    for ch in range(4):
        first = [gone_ref[2 * ch + c] for c in range(2)]
        second = [gtwo_ref[2 * ch + c] for c in range(2)]
        qy, qz = (jnp.where(odd, second[c], first[c]) for c in range(2))
        ry, rz = (jnp.where(odd, first[c], second[c]) for c in range(2))
        low = low + (fac_ref[2 * ch] * qy + fac_ref[2 * ch + 1] * qz)
        o = [fac_ref[8 + 3 * ch + c] for c in range(3)]
        high = high + (o[0] * (by(ry) + bz(rz)) - o[1] * ry - o[2] * rz)
    two_ref[0:NY] = low
    two_ref[NY:2 * NY] = high
    out_ref[...] = part_ref[...] + pick(hot_ref[...], two_ref[...])


def owner_kernel(got_ref, out_ref):
    codes = got_ref[pl.ds(CAP, DEV, stride=SLOTS), :]
    offs = codes.T[0:CAP].astype(I32)
    want = lax.broadcasted_iota(I32, (G_DEV, DEV), 0) + 1
    hot = jnp.concatenate([one_hot(want == offs[k:k + 1]) for k in range(CAP)], axis=1)
    out_ref[...] = pick(hot, jnp.concatenate([got_ref[pl.ds(k, DEV, stride=SLOTS), :] for k in range(CAP)], axis=0))


SMEM = pl.BlockSpec(memory_space=pltpu.SMEM)
VMEM = pl.BlockSpec(memory_space=pltpu.VMEM)
HBM = pl.BlockSpec(memory_space=pltpu.HBM)
LIMIT = 40 * 1024 * 1024


def f32(*shape):
    return jax.ShapeDtypeStruct(shape, F32)


def call(kernel, name, ins, outs, scratch, flops, moved):
    return pl.pallas_call(
        kernel,
        in_specs=ins,
        out_specs=[VMEM] * len(outs),
        out_shape=outs,
        scratch_shapes=scratch,
        compiler_params=pltpu.CompilerParams(vmem_limit_bytes=LIMIT),
        cost_estimate=pl.CostEstimate(flops=flops, bytes_accessed=moved, transcendentals=0),
        name=name,
    )


def per_device(fields, sources, conductivity, omegas, tx_bricks, owner_map, row_brick, row_offset):
    fields_in, sources_in, conductivity_in, omegas_in = fields, sources, conductivity, omegas
    fields, sources, conductivity, omegas = (
        pltpu.with_memory_space_constraint(x, pltpu.HBM) for x in (fields, sources, conductivity, omegas)
    )
    with_next = [(i, (i + 1) % BRICK) for i in range(1, BRICK, 2)]
    with_last = [(i, i + 1) for i in range(0, BRICK, 2)]
    with_next, with_last = (pairs + [(b, a) for a, b in pairs] for pairs in (with_next, with_last))
    pay = f32(8, NY, NZ)
    packed = f32(DEV * SLOTS, NZ)
    dma = pltpu.SemaphoreType.DMA
    one_e, two_e = call(
        field_halo_kernel, "field_halo", [HBM], [pay, pay],
        [pltpu.VMEM((NF, 2, 2, NY, NZ), F32), pltpu.VMEM((NF, 2, 3, NY, NZ), F32), dma((2 * NF,))], 400_000, 1_200_000,
    )(fields)
    gone_e = lax.ppermute(one_e, BRICK_AXES, with_next)
    gtwo_e = lax.ppermute(two_e, BRICK_AXES, with_last)
    one_r, two_r, slot, index = call(
        residual_halo_kernel, "residual_halo", [HBM] * 7,
        [pay, pay, jax.ShapeDtypeStruct((8, ROWS), I32), f32(DEV, NZ)],
        [
            pltpu.SMEM((NF,), F32),
            pltpu.VMEM((1, ROWS), I32),
            pltpu.VMEM((1, ROWS), I32),
            pltpu.VMEM((1, DEV), I32),
            pltpu.VMEM((NF, 2, 3, 2, NY, NZ), F32),
            pltpu.VMEM((NF, 2, 3, 2, NY, NZ), F32),
            pltpu.VMEM((NF, 2, 2, NY, NZ), F32),
            pltpu.VMEM((NF, 2, 3, NY, NZ), F32),
            pltpu.VMEM((2, NY, NZ), F32),
            dma((14,)),
        ], 2_000_000, 3_000_000,
    )(
        omegas, fields, sources, conductivity,
        *(
            pltpu.with_memory_space_constraint(x, pltpu.HBM)
            for x in (row_brick.reshape(1, ROWS), row_offset, owner_map.reshape(1, DEV))
        ),
    )
    gone_r = lax.ppermute(one_r, BRICK_AXES, with_next)
    gtwo_r = lax.ppermute(two_r, BRICK_AXES, with_last)
    fields_v, sources_v, conductivity_v, _ = lax.optimization_barrier((fields_in, sources_in, conductivity_in, two_r))
    fields_v, sources_v, conductivity_v = (
        pltpu.with_memory_space_constraint(x, pltpu.VMEM) for x in (fields_v, sources_v, conductivity_v)
    )
    halo = [pltpu.VMEM((8, PAD + NY, NZ), F32), pltpu.VMEM((4, NY, NZ), F32)]
    (r,) = call(
        residual_kernel, "residual", [SMEM] + [VMEM] * 3, [f32(12, PL + 1, NY + PAD, NZ)], halo, 30_000_000, 8_000_000,
    )(omegas_in, fields_v, sources_v, conductivity_v)
    part, rest, fac, hot, _ = pl.pallas_call(
        adjoint_kernel,
        in_specs=[SMEM, SMEM] + [VMEM] * 7,
        out_specs=[VMEM] * 5,
        out_shape=[packed, f32(2, NY, NZ), f32(20, NY, NZ), jax.ShapeDtypeStruct((DEV * SLOTS, 2 * NY), BF16), f32(12, PL + 1, NY + PAD, NZ)],
        input_output_aliases={8: 4},
        scratch_shapes=halo + [pltpu.VMEM((ROWS, NZ), F32)],
        compiler_params=pltpu.CompilerParams(vmem_limit_bytes=LIMIT),
        cost_estimate=pl.CostEstimate(flops=40_000_000, bytes_accessed=8_000_000, transcendentals=0),
        name="adjoint",
    )(omegas_in, tx_bricks, fields_v, conductivity_v, slot, index, gone_e, gtwo_e, r)
    (send,) = call(
        residual_fix_kernel, "residual_fix", [VMEM] * 6, [packed], [pltpu.VMEM((2 * NY, NZ), F32)], 20_000_000, 3_000_000,
    )(fac, rest, gone_r, gtwo_r, hot, part)
    got = lax.all_to_all(send.reshape(DEV, 1, SLOTS * NZ), SWAP_AXES, 0, 0, tiled=True).reshape(DEV * SLOTS, NZ)
    return pl.pallas_call(
        owner_kernel,
        in_specs=[VMEM],
        out_specs=VMEM,
        out_shape=f32(G_DEV, NZ),
        compiler_params=pltpu.CompilerParams(vmem_limit_bytes=LIMIT),
        name="owner_sum",
    )(got)


def solution(mesh):
    grid = Mesh(mesh.devices.reshape(4, 2, 4, 4), ("y", "core", "x", "z"))
    return jax.shard_map(
        per_device,
        mesh=grid,
        in_specs=(
            P(TX_AXES, None, None, None, BRICK_AXES, None, None),
            P(TX_AXES, None, None, None, BRICK_AXES, None, None),
            P(TX_AXES, BRICK_AXES, None, None),
            P(),
            P(),
            P(),
            P(TX_AXES, BRICK_AXES, None),
            P(TX_AXES, BRICK_AXES),
        ),
        out_specs=P(TX_AXES + BRICK_AXES, None),
        check_vma=False,
    )
```

```python
import jax
import jax.numpy as jnp
from jax import lax
from jax.experimental import pallas as pl
from jax.experimental.pallas import tpu as pltpu
from jax.sharding import Mesh, PartitionSpec as P

PL, NY, NZ, NF = 8, 64, 128, 2
ROWS = PL * NY
G_DEV = 32
CAP = 8
DEV = 128
SLOTS = CAP + 1
BRICK = 16
TX_AXES, BRICK_AXES = ("y", "core"), ("x", "z")
SWAP_AXES = ("core", "y", "x", "z")
PAD = 8
CH = 16
F32, BF16, I32 = jnp.float32, jnp.bfloat16, jnp.int32
SCALE = 0.003


def fy(v):
    rows = lax.broadcasted_iota(I32, v.shape, 0)
    return jnp.where(rows == NY - 1, 0.0, pltpu.roll(v, NY - 1, 0)) - v


def by(v):
    rows = lax.broadcasted_iota(I32, v.shape, 0)
    return v - jnp.where(rows == 0, 0.0, pltpu.roll(v, 1, 0))


def fz(v):
    lanes = lax.broadcasted_iota(I32, v.shape, 1)
    return jnp.where(lanes == NZ - 1, 0.0, pltpu.roll(v, NZ - 1, 1)) - v


def bz(v):
    lanes = lax.broadcasted_iota(I32, v.shape, 1)
    return v - jnp.where(lanes == 0, 0.0, pltpu.roll(v, 1, 1))


def q_of(vx, vy, vz):
    return fz(vx) + vz, vy + fy(vx)


def rotate(curl, part, weight, other):
    return curl - weight * other if part == 0 else curl + weight * other


def signed(part, value):
    return value if part == 1 else -value


def odd_brick():
    return (lax.axis_index(BRICK_AXES) & 1) == 1


def field_halo_kernel(e_hbm, one_ref, two_ref, lo_ref, hi_ref, sems):
    odd = odd_brick()
    hi = pltpu.make_async_copy(e_hbm.at[0, :, :, :, PL - 1], hi_ref, sems.at[0])
    lo = pltpu.make_async_copy(e_hbm.at[0, :, :, pl.ds(1, 2), 0], lo_ref, sems.at[1])
    hi.start()
    lo.start()
    hi.wait()
    lo.wait()
    for f in range(NF):
        for part in range(2):
            q = q_of(*(hi_ref[f, part, c] for c in range(3)))
            for c in range(2):
                at = 2 * (2 * f + part) + c
                one_ref[at] = jnp.where(odd, q[c], lo_ref[f, part, c])
                two_ref[at] = jnp.where(odd, lo_ref[f, part, c], q[c])


def one_hot(cond):
    return jnp.where(cond, 1.0, 0.0).astype(BF16)


def dot(a, b):
    return jnp.dot(a, b, preferred_element_type=F32)


def row_slots(rb_ref, ro_ref, own_ref, slot_ref, index_ref):
    bt = lax.broadcasted_iota(I32, (DEV, ROWS), 0) == rb_ref[...]
    hot = one_hot(bt)
    before = one_hot(lax.broadcasted_iota(I32, (ROWS, ROWS), 0) < lax.broadcasted_iota(I32, (ROWS, ROWS), 1))
    counts = dot(hot, before)
    rank = jnp.sum(jnp.where(bt, counts, 0.0), axis=0, keepdims=True)
    own8 = jnp.broadcast_to(own_ref[...].astype(F32), (8, DEV)).astype(BF16)
    dest = dot(own8, hot)[0:1].astype(I32)
    dest = (dest & 3) * 1 + ((dest >> 2) & 3) * 4 + (dest >> 5) * 16 + ((dest >> 4) & 1) * 64
    rank = rank.astype(I32)
    slot = dest * SLOTS + rank
    slot_ref[...] = jnp.broadcast_to(slot, (8, ROWS))
    codes = jnp.where(lax.broadcasted_iota(I32, (NZ, ROWS), 0) == rank, (ro_ref[...] + 1).astype(F32), 0.0).astype(BF16)
    mine = one_hot(lax.broadcasted_iota(I32, (DEV, ROWS), 0) == dest)
    index_ref[...] = lax.dot_general(mine, codes, (((1,), (1,)), ((), ())), preferred_element_type=F32)


def residual_halo_kernel(
    om_hbm, e_hbm, s_hbm, c_hbm, rb_hbm, ro_hbm, own_hbm, one_ref, two_ref, slot_ref, index_ref,
    om_ref, rb_ref, ro_ref, own_ref, elo_ref, ehi_ref, slo_ref, shi_ref, cc_ref, sems,
):
    odd = odd_brick()
    few = [
        pltpu.make_async_copy(rb_hbm, rb_ref, sems.at[8]),
        pltpu.make_async_copy(ro_hbm, ro_ref, sems.at[9]),
        pltpu.make_async_copy(own_hbm, own_ref, sems.at[10]),
        pltpu.make_async_copy(om_hbm, om_ref, sems.at[11]),
        pltpu.make_async_copy(c_hbm.at[0, 0], cc_ref.at[0], sems.at[12]),
        pltpu.make_async_copy(c_hbm.at[0, PL - 1], cc_ref.at[1], sems.at[13]),
    ]
    big = [
        [
            pltpu.make_async_copy(e_hbm.at[0, f, :, :, pl.ds(PL - 2, 2)], ehi_ref.at[f], sems.at[4 * f]),
            pltpu.make_async_copy(s_hbm.at[0, f, :, :, PL - 1], shi_ref.at[f], sems.at[4 * f + 1]),
            pltpu.make_async_copy(e_hbm.at[0, f, :, :, pl.ds(0, 2)], elo_ref.at[f], sems.at[4 * f + 2]),
            pltpu.make_async_copy(s_hbm.at[0, f, :, pl.ds(1, 2), 0], slo_ref.at[f], sems.at[4 * f + 3]),
        ]
        for f in range(NF)
    ]
    for copy in few + big[0] + big[1]:
        copy.start()
    for copy in few:
        copy.wait()
    row_slots(rb_ref, ro_ref, own_ref, slot_ref, index_ref)
    for f in range(NF):
        om = om_ref[f]
        big[f][0].wait()
        big[f][1].wait()
        for part in range(2):
            ch = 2 * f + part
            ux, uy, uz = (ehi_ref[f, part, c, 0] for c in range(3))
            vx, vy, vz = (ehi_ref[f, part, c, 1] for c in range(3))
            hy, qz = q_of(vx, vy, vz)
            hz = -qz
            hx = fy(vz) - fz(vy)
            gy = fz(ux) - (vz - uz)
            gz = (vy - uy) - fy(ux)
            w = om * cc_ref[1]
            o = [ehi_ref[f, 1 - part, c, 1] for c in range(3)]
            rx = rotate(by(hz) - bz(hy), part, w, o[0]) - shi_ref[f, part, 0]
            ry = rotate(bz(hx) - (hz - gz), part, w, o[1]) - shi_ref[f, part, 1]
            rz = rotate((hy - gy) - by(hx), part, w, o[2]) - shi_ref[f, part, 2]
            one_ref[2 * ch], one_ref[2 * ch + 1] = q_of(rx, ry, rz)
        big[f][2].wait()
        big[f][3].wait()
        for part in range(2):
            ch = 2 * f + part
            vx, vy, vz = (elo_ref[f, part, c, 0] for c in range(3))
            hx = fy(vz) - fz(vy)
            hy = fz(vx) - (elo_ref[f, part, 2, 1] - vz)
            hz = (elo_ref[f, part, 1, 1] - vy) - fy(vx)
            w = om * cc_ref[0]
            dn = [
                rotate(bz(hx) - hz, part, w, elo_ref[f, 1 - part, 1, 0]) - slo_ref[f, part, 0],
                rotate(hy - by(hx), part, w, elo_ref[f, 1 - part, 2, 0]) - slo_ref[f, part, 1],
            ]
            for c in range(2):
                up = one_ref[2 * ch + c]
                one_ref[2 * ch + c] = jnp.where(odd, up, dn[c])
                two_ref[2 * ch + c] = jnp.where(odd, dn[c], up)


def pick(hot, v):
    hi = v.astype(BF16)
    low = (v - hi.astype(F32)).astype(BF16)
    both = dot(hot, jnp.concatenate([hi, low], axis=1))
    return both[:, 0:NZ] + both[:, NZ:2 * NZ]


def place(tb_ref):
    brick = lax.axis_index(BRICK_AXES)
    span = tb_ref[lax.axis_index(TX_AXES)]
    live = jnp.where(brick < span, 1.0, 0.0).astype(F32)
    low = jnp.where(brick > 0, 1.0, 0.0).astype(F32)
    nxt = jnp.where(brick + 1 < span, 1.0, 0.0).astype(F32)
    return live, low, nxt


def curl(get, h_ref, g_ref, p, y, ch):
    lanes = lax.broadcasted_iota(I32, (CH, NZ), 1)

    def nz_(v):
        return jnp.where(lanes == NZ - 1, 0.0, pltpu.roll(v, NZ - 1, 1))

    def pz_(v):
        return jnp.where(lanes == 0, 0.0, pltpu.roll(v, 1, 1))

    vx, vy, vz = (get(c, p, y) for c in range(3))
    hx = (get(2, p, y + 1) - vz) - (nz_(vy) - vy)
    hy = (nz_(vx) - vx) - (get(2, p + 1, y) - vz)
    hz = (get(1, p + 1, y) - vy) - (get(0, p, y + 1) - vx)
    gy = g_ref[ch, y:y + CH]
    gz = h_ref[2 * ch + 1, PAD + y:PAD + y + CH]
    h_ref[2 * ch, PAD + y:PAD + y + CH] = hx
    h_ref[2 * ch + 1, PAD + y:PAD + y + CH] = hz
    g_ref[ch, y:y + CH] = hy
    hxp = h_ref[2 * ch, PAD + y - 1:PAD + y - 1 + CH]
    hzp = h_ref[2 * ch + 1, PAD + y - 1:PAD + y - 1 + CH]
    cx = (hz - hzp) - (hy - pz_(hy))
    cy = (hx - pz_(hx)) - (hz - gz)
    cz = (hy - gy) - (hx - hxp)
    return (vx, vy, vz), (cx, cy, cz)


def residual_kernel(om_ref, e_ref, s_ref, c_ref, r_ref, h_ref, g_ref):
    zero = jnp.zeros((NY, NZ), F32)
    zpad = jnp.zeros((PAD, NZ), F32)
    for i in range(12):
        for p in range(PL):
            r_ref[i, p, NY:NY + PAD] = zpad
    for i in range(8):
        h_ref[i, 0:PAD] = zpad
        h_ref[i, PAD:PAD + NY] = zero
    for i in range(4):
        g_ref[i] = zero

    rows = lax.broadcasted_iota(I32, (CH, NZ), 0)

    def step(p, carry):
        after = jnp.minimum(p + 1, PL - 1)
        inside = jnp.where(p < PL - 1, 1.0, 0.0).astype(F32)
        for y in range(0, NY, CH):
            sig = c_ref[0, p, y:y + CH]
            for f in range(NF):
                w = om_ref[f] * sig
                for part in range(2):
                    ch = 2 * f + part

                    def get(c, q, r):
                        if q is not p:
                            return e_ref[0, f, part, c, after, r:r + CH] * inside
                        if r + CH <= NY:
                            return e_ref[0, f, part, c, p, r:r + CH]
                        last = e_ref[0, f, part, c, p, NY - CH:NY]
                        return jnp.where(rows == CH - 1, 0.0, pltpu.roll(last, CH - 1, 0))

                    _, cs = curl(get, h_ref, g_ref, p, y, ch)
                    for c in range(3):
                        o = e_ref[0, f, 1 - part, c, p, y:y + CH]
                        r_ref[3 * ch + c, p, y:y + CH] = rotate(cs[c], part, w, o) - s_ref[0, f, part, c, p, y:y + CH]
        return carry

    lax.fori_loop(0, PL, step, 0)
    for ch in range(4):
        r_ref[3 * ch + 1, PL, 0:NY] = h_ref[2 * ch + 1, PAD:PAD + NY]
        r_ref[3 * ch + 2, PL, 0:NY] = -g_ref[ch]


def adjoint_kernel(
    om_ref, tb_ref, e_ref, c_ref, slot_ref, index_ref, gone_ref, gtwo_ref, rin_ref,
    part_ref, rest_ref, fac_ref, hot_ref, r_ref, h_ref, g_ref, loc_ref,
):
    live, low, nxt = place(tb_ref)
    odd = odd_brick()
    end = PL - 1
    zpad = jnp.zeros((PAD, NZ), F32)
    for i in range(8):
        h_ref[i, 0:PAD] = zpad
    for f in range(NF):
        weight = SCALE * om_ref[f] * live
        for part in range(2):
            ch = 2 * f + part
            x, y, z = 3 * ch, 3 * ch + 1, 3 * ch + 2
            ey, ez = e_ref[0, f, part, 1, 0], e_ref[0, f, part, 2, 0]
            first = [gone_ref[2 * ch + c] for c in range(2)]
            second = [gtwo_ref[2 * ch + c] for c in range(2)]
            qy, qz = (jnp.where(odd, second[c], first[c]) for c in range(2))
            ry = rin_ref[y, 0, 0:NY] + low * (ey - qz)
            rz = rin_ref[z, 0, 0:NY] + low * (ez - qy)
            r_ref[y, 0, 0:NY] = ry
            r_ref[z, 0, 0:NY] = rz
            div = by(ey) + bz(ez)
            g_ref[ch] = low * (fz(div) - ez - rz)
            h_ref[2 * ch + 1, PAD:PAD + NY] = low * (ry - fy(div) + ey)
            ey, ez = (nxt * jnp.where(odd, first[c], second[c]) for c in range(2))
            r_ref[x, end, 0:NY] = rin_ref[x, end, 0:NY] + (by(ey) + bz(ez))
            r_ref[y, end, 0:NY] = rin_ref[y, end, 0:NY] - ey
            r_ref[z, end, 0:NY] = rin_ref[z, end, 0:NY] - ez
            r_ref[y, PL, 0:NY] = nxt * rin_ref[y, PL, 0:NY] + ey
            r_ref[z, PL, 0:NY] = nxt * rin_ref[z, PL, 0:NY] + ez
            scale = -signed(part, weight) * low
            fac_ref[2 * ch] = scale * e_ref[0, f, 1 - part, 2, 0]
            fac_ref[2 * ch + 1] = scale * e_ref[0, f, 1 - part, 1, 0]
            scale = signed(part, weight) * nxt
            for c in range(3):
                fac_ref[8 + 3 * ch + c] = scale * e_ref[0, f, 1 - part, c, end]

    def step(p, carry):
        for y in range(0, NY, CH):
            sig = c_ref[0, p, y:y + CH]
            acc = jnp.zeros((CH, NZ), F32)
            for f in range(NF):
                om = om_ref[f]
                tot = jnp.zeros((CH, NZ), F32)
                dia = jnp.zeros((CH, NZ), F32)
                for part in range(2):
                    ch = 2 * f + part
                    vs, cs = curl(lambda c, q, r: r_ref[3 * ch + c, q, r:r + CH], h_ref, g_ref, p, y, ch)
                    o = [e_ref[0, f, 1 - part, c, p, y:y + CH] for c in range(3)]
                    s = [e_ref[0, f, part, c, p, y:y + CH] for c in range(3)]
                    tot = tot + signed(part, o[0] * cs[0] + o[1] * cs[1] + o[2] * cs[2])
                    dia = dia + (s[0] * vs[0] + s[1] * vs[1] + s[2] * vs[2])
                acc = acc + (SCALE * om * live) * (tot + (om * sig) * dia)
            loc_ref[pl.ds(pl.multiple_of(p * NY + y, CH), CH), :] = acc
        return carry

    lax.fori_loop(0, PL, step, 0)

    ends = lax.broadcasted_iota(I32, (DEV * SLOTS, NY), 0)
    hot_ref[...] = jnp.concatenate(
        [one_hot(ends == slot_ref[0:1, 0:NY]), one_hot(ends == slot_ref[0:1, ROWS - NY:ROWS])], axis=1
    )
    rest_ref[0] = loc_ref[0:NY]
    rest_ref[1] = loc_ref[ROWS - NY:ROWS]
    lo, hi = NY, ROWS - NY
    at = lax.broadcasted_iota(I32, (DEV * SLOTS, hi - lo), 0)
    part_ref[...] = pick(one_hot(at == slot_ref[0:1, lo:hi]), loc_ref[lo:hi])
    part_ref[pl.ds(CAP, DEV, stride=SLOTS), :] = index_ref[...]


def residual_fix_kernel(fac_ref, rest_ref, gone_ref, gtwo_ref, hot_ref, part_ref, out_ref):
    odd = odd_brick()
    low, high = rest_ref[0], rest_ref[1]
    for ch in range(4):
        first = [gone_ref[2 * ch + c] for c in range(2)]
        second = [gtwo_ref[2 * ch + c] for c in range(2)]
        qy, qz = (jnp.where(odd, second[c], first[c]) for c in range(2))
        ry, rz = (jnp.where(odd, first[c], second[c]) for c in range(2))
        low = low + (fac_ref[2 * ch] * qy + fac_ref[2 * ch + 1] * qz)
        o = [fac_ref[8 + 3 * ch + c] for c in range(3)]
        high = high + (o[0] * (by(ry) + bz(rz)) - o[1] * ry - o[2] * rz)
    out_ref[...] = part_ref[...] + pick(hot_ref[...], jnp.concatenate([low, high], axis=0))


def owner_kernel(got_ref, out_ref):
    codes = got_ref[pl.ds(CAP, DEV, stride=SLOTS), :]
    offs = codes.T[0:CAP].astype(I32)
    want = lax.broadcasted_iota(I32, (G_DEV, DEV), 0) + 1
    hot = jnp.concatenate([one_hot(want == offs[k:k + 1]) for k in range(CAP)], axis=1)
    out_ref[...] = pick(hot, jnp.concatenate([got_ref[pl.ds(k, DEV, stride=SLOTS), :] for k in range(CAP)], axis=0))


SMEM = pl.BlockSpec(memory_space=pltpu.SMEM)
VMEM = pl.BlockSpec(memory_space=pltpu.VMEM)
HBM = pl.BlockSpec(memory_space=pltpu.HBM)
LIMIT = 40 * 1024 * 1024


def f32(*shape):
    return jax.ShapeDtypeStruct(shape, F32)


def call(kernel, name, ins, outs, scratch, flops, moved):
    return pl.pallas_call(
        kernel,
        in_specs=ins,
        out_specs=[VMEM] * len(outs),
        out_shape=outs,
        scratch_shapes=scratch,
        compiler_params=pltpu.CompilerParams(vmem_limit_bytes=LIMIT),
        cost_estimate=pl.CostEstimate(flops=flops, bytes_accessed=moved, transcendentals=0),
        name=name,
    )


def per_device(fields, sources, conductivity, omegas, tx_bricks, owner_map, row_brick, row_offset):
    fields_in, sources_in, conductivity_in, omegas_in = fields, sources, conductivity, omegas
    fields, sources, conductivity, omegas = (
        pltpu.with_memory_space_constraint(x, pltpu.HBM) for x in (fields, sources, conductivity, omegas)
    )
    with_next = [(i, (i + 1) % BRICK) for i in range(1, BRICK, 2)]
    with_last = [(i, i + 1) for i in range(0, BRICK, 2)]
    with_next, with_last = (pairs + [(b, a) for a, b in pairs] for pairs in (with_next, with_last))
    pay = f32(8, NY, NZ)
    packed = f32(DEV * SLOTS, NZ)
    dma = pltpu.SemaphoreType.DMA
    one_e, two_e = call(
        field_halo_kernel, "field_halo", [HBM], [pay, pay],
        [pltpu.VMEM((NF, 2, 2, NY, NZ), F32), pltpu.VMEM((NF, 2, 3, NY, NZ), F32), dma((2 * NF,))], 400_000, 1_200_000,
    )(fields)
    gone_e = lax.ppermute(one_e, BRICK_AXES, with_next)
    gtwo_e = lax.ppermute(two_e, BRICK_AXES, with_last)
    one_r, two_r, slot, index = call(
        residual_halo_kernel, "residual_halo", [HBM] * 7,
        [pay, pay, jax.ShapeDtypeStruct((8, ROWS), I32), f32(DEV, NZ)],
        [
            pltpu.SMEM((NF,), F32),
            pltpu.VMEM((1, ROWS), I32),
            pltpu.VMEM((1, ROWS), I32),
            pltpu.VMEM((1, DEV), I32),
            pltpu.VMEM((NF, 2, 3, 2, NY, NZ), F32),
            pltpu.VMEM((NF, 2, 3, 2, NY, NZ), F32),
            pltpu.VMEM((NF, 2, 2, NY, NZ), F32),
            pltpu.VMEM((NF, 2, 3, NY, NZ), F32),
            pltpu.VMEM((2, NY, NZ), F32),
            dma((14,)),
        ], 2_000_000, 3_000_000,
    )(
        omegas, fields, sources, conductivity,
        *(
            pltpu.with_memory_space_constraint(x, pltpu.HBM)
            for x in (row_brick.reshape(1, ROWS), row_offset, owner_map.reshape(1, DEV))
        ),
    )
    gone_r = lax.ppermute(one_r, BRICK_AXES, with_next)
    gtwo_r = lax.ppermute(two_r, BRICK_AXES, with_last)
    fields_v, sources_v, conductivity_v, _ = lax.optimization_barrier((fields_in, sources_in, conductivity_in, two_r))
    fields_v, sources_v, conductivity_v = (
        pltpu.with_memory_space_constraint(x, pltpu.VMEM) for x in (fields_v, sources_v, conductivity_v)
    )
    halo = [pltpu.VMEM((8, PAD + NY, NZ), F32), pltpu.VMEM((4, NY, NZ), F32)]
    (r,) = call(
        residual_kernel, "residual", [SMEM] + [VMEM] * 3, [f32(12, PL + 1, NY + PAD, NZ)], halo, 30_000_000, 8_000_000,
    )(omegas_in, fields_v, sources_v, conductivity_v)
    part, rest, fac, hot, _ = pl.pallas_call(
        adjoint_kernel,
        in_specs=[SMEM, SMEM] + [VMEM] * 7,
        out_specs=[VMEM] * 5,
        out_shape=[packed, f32(2, NY, NZ), f32(20, NY, NZ), jax.ShapeDtypeStruct((DEV * SLOTS, 2 * NY), BF16), f32(12, PL + 1, NY + PAD, NZ)],
        input_output_aliases={8: 4},
        scratch_shapes=halo + [pltpu.VMEM((ROWS, NZ), F32)],
        compiler_params=pltpu.CompilerParams(vmem_limit_bytes=LIMIT),
        cost_estimate=pl.CostEstimate(flops=40_000_000, bytes_accessed=8_000_000, transcendentals=0),
        name="adjoint",
    )(omegas_in, tx_bricks, fields_v, conductivity_v, slot, index, gone_e, gtwo_e, r)
    (send,) = call(
        residual_fix_kernel, "residual_fix", [VMEM] * 6, [packed], [], 20_000_000, 3_000_000,
    )(fac, rest, gone_r, gtwo_r, hot, part)
    got = lax.all_to_all(send.reshape(DEV, 1, SLOTS * NZ), SWAP_AXES, 0, 0, tiled=True).reshape(DEV * SLOTS, NZ)
    return pl.pallas_call(
        owner_kernel,
        in_specs=[VMEM],
        out_specs=VMEM,
        out_shape=f32(G_DEV, NZ),
        compiler_params=pltpu.CompilerParams(vmem_limit_bytes=LIMIT),
        name="owner_sum",
    )(got)


def solution(mesh):
    grid = Mesh(mesh.devices.reshape(4, 2, 4, 4), ("y", "core", "x", "z"))
    return jax.shard_map(
        per_device,
        mesh=grid,
        in_specs=(
            P(TX_AXES, None, None, None, BRICK_AXES, None, None),
            P(TX_AXES, None, None, None, BRICK_AXES, None, None),
            P(TX_AXES, BRICK_AXES, None, None),
            P(),
            P(),
            P(),
            P(TX_AXES, BRICK_AXES, None),
            P(TX_AXES, BRICK_AXES),
        ),
        out_specs=P(TX_AXES + BRICK_AXES, None),
        check_vma=False,
    )
```
